32 devices in a mesh: blk: 8 (over z, y), tp: 4 (over x, core).
Axes of the slice: x: 2, y: 2, z: 4, core: 2. Of those that a mesh axis runs over, the one named last changes fastest.
Arguments:
- queries: bfloat16 [8192, 1664], P(('blk', 'tp')), may hold values from -120 to 120
- keys: bfloat16 [8192, 1664], P(('blk', 'tp')), may hold values from -6 to 6
- values: bfloat16 [8192, 1664], P(('blk', 'tp')), may hold values from -6 to 6
- segment_ids: int32 [8192], replicated, may hold values from -1 to 7, as said below
- proj_weight: bfloat16 [6656, 3072], P(None, 'tp'), may hold values from -0.078125 to 0.078125
Outputs:
- normed: bfloat16 [2048, 3072], P('blk', 'tp')
- seg_peaks: float32 [8], replicated
The draws below stay inside these ranges and needn't reach their ends.
Inputs may be any that keep to these rules, and one draw needn't show every extreme that they name: `segment_ids`: ids other than -1 never fall along the pack; every image 0 to 7 occurs as one run of tokens that starts at a multiple of 4 and has a multiple of 4 tokens, at most 1024; some image has exactly 1024; -1 marks padding tokens, which may stand between images.
All inputs are finite; a program needn't handle non-finite values.
Results may differ from the reference program's by a relative error of at most 0.0056.
Values may be sent and summed in bfloat16 or wider, within the bound.
A program may use at most 128 MiB of HBM per device.

```python
import jax
import jax.numpy as jnp
from jax import lax

TOK_DEV = 1024
HEAD = 128
NOUT = 3072
HD = 1664
MERGED = 6656
TOKENS = 8192
MROWS = 2048
SEGS = 8
MOST = 256
N_BLK = 8


def shared_rows(key):
    key_rows = jnp.clip(jax.random.normal(jax.random.fold_in(key, 101), (TOKENS, HD), jnp.float32), -6.0, 6.0)
    query_rows = jnp.clip(jax.random.normal(jax.random.fold_in(key, 202), (TOKENS, HD), jnp.float32), -6.0, 6.0)
    return (query_rows, key_rows)


def draw_queries(key, part):
    return shared_rows(key)[0].astype(jnp.bfloat16)


def draw_keys(key, part):
    return shared_rows(key)[1].astype(jnp.bfloat16)


def draw_segment_ids(key, part):
    first_key, second_key, third_key = jax.random.split(jax.random.fold_in(key, 7), 3)
    least = max(1, MOST // 8)
    quarter = MOST // 4
    image_index = jnp.arange(SEGS, dtype=jnp.int32)
    chosen = jax.random.randint(third_key, (), 1, SEGS, dtype=jnp.int32)
    heads_part = jax.random.randint(first_key, (SEGS,), least, MOST - least + 1, dtype=jnp.int32)
    heads_part = jnp.where(image_index == chosen, quarter, heads_part)
    heads_part = jnp.where(image_index == chosen - 1, jnp.minimum(heads_part, quarter), heads_part)
    heads_before = jnp.concatenate([jnp.zeros((1,), jnp.int32), heads_part[:-1]])
    tail_cap = jnp.minimum(MOST - heads_before, MOST - heads_part)
    tails_part = jax.random.randint(second_key, (SEGS,), least, tail_cap + 1, dtype=jnp.int32)
    tails_part = jnp.where(image_index == chosen, MOST - quarter, tails_part)
    tails_part = jnp.where(image_index == 0, 0, tails_part)
    position = jnp.arange(MROWS, dtype=jnp.int32)
    block = position // MOST
    offset = position % MOST
    next_image = jnp.minimum(block + 1, SEGS - 1)
    head_len = jnp.take(heads_part, block)
    tail_len = jnp.take(tails_part, next_image)
    in_head = offset < head_len
    in_tail = (offset >= MOST - tail_len) & (block + 1 < SEGS)
    merged_ids = jnp.where(in_head, block, jnp.where(in_tail, block + 1, -1))
    return jnp.repeat(merged_ids.astype(jnp.int32), 4)


def levels(rng, shape, cuts, low, largest):
    gain, own = 1.0, jax.random.fold_in(rng, 6)
    for axis_at, parts in cuts:
        heights = jnp.exp(jax.random.uniform(jax.random.fold_in(own, axis_at), (parts,), jnp.float32, low / len(cuts), largest / len(cuts)))
        gain = gain * jnp.repeat(heights, shape[axis_at] // parts).reshape([-1 if axis == axis_at else 1 for axis in range(len(shape))])
    return gain


def gaussian(rng, shape, scale, bound, pieces=(), held_as=jnp.bfloat16):
    loudness = levels(rng, shape, pieces, -0.22, 0.18) if pieces else 1.0
    values = jax.random.normal(rng, shape, jnp.float32) * scale * loudness
    return jnp.minimum(jnp.maximum(values, -bound), bound).astype(held_as)


def setup_inputs(seed: int = 0) -> dict:
    key_list = jax.random.split(jax.random.key(seed), 6)
    return {
        "queries": draw_queries(jax.random.fold_in(key_list[5], 71), 0),
        "keys": draw_keys(jax.random.fold_in(key_list[5], 71), 0),
        "values": gaussian(key_list[2], (TOKENS, HD), 1.0, 6.0, ((0, 32),)),
        "segment_ids": draw_segment_ids(jax.random.fold_in(key_list[5], 71), 0),
        "proj_weight": gaussian(key_list[4], (MERGED, NOUT), MERGED ** -0.5, 0.078125, ((1, 4),)),
    }


masked_score = -1e+30
epsilon = 1e-06

def finish(scores, allowed, value_heads):
    scores = jnp.where(allowed[None], scores, masked_score)
    row_top = lax.optimization_barrier(jnp.max(scores, axis=2, keepdims=True))
    exp_terms = jnp.where(allowed[None], jnp.exp(scores - row_top), 0.0)
    row_total = jnp.maximum(lax.optimization_barrier(jnp.sum(exp_terms, axis=2)), 1.0)
    weights = exp_terms.astype(jnp.bfloat16).astype(jnp.float32)
    mixed_out = jnp.einsum('hrk,khd->rhd', weights, value_heads.astype(jnp.float32))
    return mixed_out / row_total.T[:, :, None]

def reference(queries, keys, values, segment_ids, proj_weight):
    heads_count = queries.shape[1] // HEAD
    zero_rows = jnp.zeros((TOK_DEV, queries.shape[1]), jnp.bfloat16)
    padded_keys = jnp.concatenate([zero_rows, keys, zero_rows], axis=0)
    padded_values = jnp.concatenate([zero_rows, values, zero_rows], axis=0)
    edge_segs = jnp.full((TOK_DEV,), -2, jnp.int32)
    padded_segs = jnp.concatenate([edge_segs, segment_ids, edge_segs], axis=0)

    def one_block(index):
        first_row = (index * TOK_DEV).astype(jnp.int32)
        query_rows = lax.dynamic_slice_in_dim(queries, first_row, TOK_DEV)
        query_segs = lax.dynamic_slice_in_dim(segment_ids, first_row, TOK_DEV)
        key_rows = lax.dynamic_slice_in_dim(padded_keys, first_row, 3 * TOK_DEV)
        value_rows = lax.dynamic_slice_in_dim(padded_values, first_row, 3 * TOK_DEV)
        key_segs = lax.dynamic_slice_in_dim(padded_segs, first_row, 3 * TOK_DEV)
        query_heads = query_rows.reshape(TOK_DEV, heads_count, HEAD).astype(jnp.float32)
        key_heads = key_rows.reshape(3 * TOK_DEV, heads_count, HEAD).astype(jnp.float32)
        value_heads = value_rows.reshape(3 * TOK_DEV, heads_count, HEAD)
        scores = jnp.einsum('rhd,khd->hrk', query_heads, key_heads) * HEAD ** (-0.5)
        allowed = (query_segs[:, None] == key_segs[None, :]) & (query_segs[:, None] >= 0)
        mixed_out = finish(scores, allowed, value_heads)
        return mixed_out.reshape(TOK_DEV, heads_count * HEAD).astype(jnp.bfloat16)
    attended = lax.map(one_block, jnp.arange(N_BLK, dtype=jnp.int32))
    attended = attended.reshape(TOKENS, queries.shape[1])
    merged = attended.reshape(MROWS, 4 * queries.shape[1])
    projected = jnp.dot(merged, proj_weight, preferred_element_type=jnp.float32)
    row_segs = segment_ids[::4]
    member = row_segs[:, None] == jnp.arange(SEGS, dtype=jnp.int32)[None, :]
    squares = lax.optimization_barrier(jnp.sum(projected * projected, axis=1))
    seg_sums = lax.optimization_barrier(jnp.sum(jnp.where(member, squares[:, None], 0.0), axis=0))
    seg_counts = lax.optimization_barrier(jnp.sum(member.astype(jnp.float32), axis=0)) * projected.shape[1]
    row_peak = lax.optimization_barrier(jnp.max(jnp.where(member, lax.optimization_barrier(jnp.max(projected, axis=1))[:, None], masked_score), axis=0))
    seg_scale = lax.rsqrt(seg_sums / seg_counts + epsilon)
    row_scale = lax.optimization_barrier(jnp.sum(jnp.where(member, seg_scale[None, :], 0.0), axis=1))
    normed = (projected * row_scale[:, None]).astype(jnp.bfloat16)
    return (normed, row_peak * seg_scale)
```

```python
import functools

import jax
import jax.numpy as jnp
from jax import lax
from jax.experimental import pallas as pl
from jax.experimental.pallas import tpu as pltpu
from jax.sharding import PartitionSpec as P

HEAD = 128
MERGE = 4
QUERY_TILE = 256
KEY_TILE = 512
LANES = 128
masked_score = -1e30
least_top = -1e20
epsilon = 1e-06
score_scale = HEAD ** (-0.5) * 1.4426950408889634
MESH = pl.DeviceIdType.MESH


def start_head(place, places, heads):
    return (place * heads) // places


def exchange_kernel(
    tp, pairs, heads, slots, block_len,
    q_ref, k_ref, v_ref, qg_ref, kg_ref, vg_ref,
    send, recv, pass_send, pass_recv, own_sem,
):
    blk, part = lax.axis_index("blk"), lax.axis_index("tp")
    side, pair = lax.rem(blk, 2), blk // 2
    places = 2 * tp
    place = side * tp + part
    rows = q_ref.shape[0]
    offsets = [(dy, dt) for dy in (1, 0) for dt in range(tp) if (dy, dt) != (0, 0)]
    arrays = ((k_ref, kg_ref, block_len), (v_ref, vg_ref, block_len), (q_ref, qg_ref, 0))
    has_prev, has_next = pair > 0, pair < pairs - 1
    n_around = jnp.minimum(pair, 1) + jnp.minimum(pairs - 1 - pair, 1)

    barrier = pltpu.get_barrier_semaphore()
    for dy, dt in offsets:
        target = (pair * 2 + lax.rem(side + dy, 2), lax.rem(part + dt, tp))
        pl.semaphore_signal(barrier, inc=1, device_id=target, device_id_type=MESH)

    @pl.when(has_prev)
    def _():
        pl.semaphore_signal(barrier, inc=1, device_id=(blk - 2, part), device_id_type=MESH)

    @pl.when(has_next)
    def _():
        pl.semaphore_signal(barrier, inc=1, device_id=(blk + 2, part), device_id_type=MESH)

    pl.semaphore_wait(barrier, len(offsets) + n_around)

    def push(a, i):
        src, dst, first = arrays[a]
        dy, dt = offsets[i]
        to_side, to_part = lax.rem(side + dy, 2), lax.rem(part + dt, tp)
        column = start_head(to_side * tp + to_part, places, heads) * HEAD
        return pltpu.make_async_remote_copy(
            src_ref=src.at[:, pl.ds(pl.multiple_of(column, HEAD), slots * HEAD)],
            dst_ref=dst.at[pl.ds(pl.multiple_of(first + place * rows, rows), rows), :],
            send_sem=send.at[a, i],
            recv_sem=recv.at[a, i],
            device_id=(pair * 2 + to_side, to_part),
            device_id_type=MESH,
        )

    def keep(a):
        src, dst, first = arrays[a]
        column = start_head(place, places, heads) * HEAD
        return pltpu.make_async_copy(
            src.at[:, pl.ds(pl.multiple_of(column, HEAD), slots * HEAD)],
            dst.at[pl.ds(pl.multiple_of(first + place * rows, rows), rows), :],
            own_sem.at[a],
        )

    def hand_on(a, forward):
        dst = arrays[a][1]
        if forward:
            src_rows, dst_rows, target = pl.ds(2 * block_len, block_len), pl.ds(0, block_len), blk + 2
        else:
            src_rows, dst_rows, target = pl.ds(block_len, block_len), pl.ds(3 * block_len, block_len), blk - 2
        return pltpu.make_async_remote_copy(
            src_ref=dst.at[src_rows, :],
            dst_ref=dst.at[dst_rows, :],
            send_sem=pass_send.at[a, forward],
            recv_sem=pass_recv.at[a, forward],
            device_id=(target, part),
            device_id_type=MESH,
        )

    def start_all(a):
        for i in range(len(offsets)):
            push(a, i).start()
        keep(a).start()

    def arrive_all(a):
        for i in range(len(offsets)):
            push(a, i).wait_recv()
        keep(a).wait()

    def hand_on_all(a):
        @pl.when(has_prev)
        def _():
            hand_on(a, 0).start()

        @pl.when(has_next)
        def _():
            hand_on(a, 1).start()

    start_all(0)
    start_all(1)
    arrive_all(0)
    hand_on_all(0)
    start_all(2)
    arrive_all(1)
    hand_on_all(1)
    arrive_all(2)
    for a in range(3):
        for i in range(len(offsets)):
            push(a, i).wait_send()
    for a in range(2):
        @pl.when(has_prev)
        def _(a=a):
            hand_on(a, 0).wait_send()
            hand_on(a, 1).wait_recv()

        @pl.when(has_next)
        def _(a=a):
            hand_on(a, 1).wait_send()
            hand_on(a, 0).wait_recv()


def attend_kernel(slots, low_ref, high_ref, q_ref, k_ref, v_ref, qs_ref, ks_ref, o_ref, mixed_ref):
    tile = pl.program_id(0)
    query_segs = qs_ref[...]
    rows = q_ref.shape[0]

    def step(chunk, carry):
        at = pl.ds(pl.multiple_of(chunk * KEY_TILE, KEY_TILE), KEY_TILE)
        same = query_segs == ks_ref[:, at]
        after = []
        for slot in range(slots):
            top, total, mixed = carry[slot]
            columns = slice(slot * HEAD, (slot + 1) * HEAD)
            scores = lax.dot_general(
                q_ref[:, columns], k_ref[at, columns], (((1,), (1,)), ((), ())),
                preferred_element_type=jnp.float32,
            )
            scores = jnp.where(same, scores, masked_score)
            new_top = jnp.maximum(top, jnp.max(scores, axis=1, keepdims=True))
            terms = jnp.exp2((scores - new_top) * score_scale)
            decay = jnp.exp2((top - new_top) * score_scale)
            total = total * decay + jnp.sum(terms, axis=1, keepdims=True)
            mixed = mixed * decay + jnp.dot(
                terms.astype(jnp.bfloat16), v_ref[at, columns], preferred_element_type=jnp.float32
            )
            after.append((new_top, total, mixed))
        return tuple(after)

    begin = tuple(
        (
            jnp.full((rows, 1), least_top, jnp.float32),
            jnp.zeros((rows, 1), jnp.float32),
            jnp.zeros((rows, HEAD), jnp.float32),
        )
        for _ in range(slots)
    )
    final = lax.fori_loop(low_ref[tile], high_ref[tile], step, begin)
    for slot in range(slots):
        _, total, mixed = final[slot]
        mixed_ref[slot] = mixed / jnp.maximum(total, 1.0)
    for slot in range(slots):
        for r in range(MERGE):
            o_ref[slot, 0, r] = mixed_ref[slot, pl.ds(r, rows // MERGE, stride=MERGE), :].astype(jnp.bfloat16)


def project_kernel(
    tp, blks, heads, slots,
    o_ref, w_ref, seg_ref, count_ref, normed_ref, peak_ref,
    merged, weight, projected, part_stats, blk_stats,
    w_sem, own_sem, y_send, y_recv, x_send, x_recv, c_send, c_recv, f_send, f_recv,
    p_send, p_recv, b_send, b_recv,
):
    blk, part = lax.axis_index("blk"), lax.axis_index("tp")
    side, place_x, core = lax.rem(blk, 2), part // 2, lax.rem(part, 2)
    x_len, places = tp // 2, 2 * tp
    here = (blk, part)
    sibling = (blk, part + 1 - 2 * core)
    across = (blk + 1 - 2 * side, part)
    load = pltpu.make_async_copy(w_ref, weight, w_sem)
    load.start()

    barrier = pltpu.get_barrier_semaphore()
    for d in range(1, tp):
        pl.semaphore_signal(barrier, inc=1, device_id=(blk, lax.rem(part + d, tp)), device_id_type=MESH)
    for d in range(1, blks):
        pl.semaphore_signal(barrier, inc=1, device_id=(lax.rem(blk + d, blks), part), device_id_type=MESH)
    pl.semaphore_wait(barrier, tp + blks - 2)

    def first(place):
        return start_head(place, places, heads)

    def held(place, slot):
        return slot < first(place + 1) - first(place)

    def place_of(kind, to_x, to_core):
        return (side if kind == 0 else 1 - side) * tp + to_x * 2 + to_core

    def copy(src, head, send_sem, recv_sem, target):
        return pltpu.make_async_remote_copy(
            src_ref=src, dst_ref=merged.at[head], send_sem=send_sem, recv_sem=recv_sem,
            device_id=target, device_id_type=MESH,
        )

    own = place_of(0, place_x, core)
    far = place_of(1, place_x, core)

    def clipped(place, slot):
        return jnp.minimum(first(place) + slot, heads - 1)

    def stay(slot):
        return pltpu.make_async_copy(o_ref.at[slot, side], merged.at[clipped(own, slot)], own_sem.at[slot])

    def go_y(slot):
        return copy(o_ref.at[slot, 1 - side], clipped(own, slot), y_send.at[slot], y_recv.at[slot], across)

    def source(kind, slot):
        return o_ref.at[slot, side] if kind == 0 else merged.at[clipped(far, slot)]

    def go_x(kind, slot, d):
        target = (blk, lax.rem(place_x + d, x_len) * 2 + core)
        head = clipped(own if kind == 0 else far, slot)
        return copy(source(kind, slot), head, x_send.at[kind, slot, d - 1], x_recv.at[kind, slot, d - 1], target)

    def go_c(kind, slot):
        head = clipped(own if kind == 0 else far, slot)
        return copy(source(kind, slot), head, c_send.at[kind, slot], c_recv.at[kind, slot], sibling)

    def go_f(kind, slot, d):
        came = clipped(place_of(kind, lax.rem(place_x + x_len - d, x_len), core), slot)
        return copy(merged.at[came], came, f_send.at[kind, slot, d - 1], f_recv.at[kind, slot, d - 1], sibling)

    slot_range, steps = range(slots), range(1, x_len)

    for slot in slot_range:
        @pl.when(held(own, slot))
        def _(slot=slot):
            go_y(slot).start()
            for d in steps:
                go_x(0, slot, d).start()
            go_c(0, slot).start()
            stay(slot).start()

    for slot in slot_range:
        @pl.when(held(far, slot))
        def _(slot=slot):
            go_y(slot).wait_recv()
            for d in steps:
                go_x(1, slot, d).start()
            go_c(1, slot).start()

    for kind in range(2):
        for d in steps:
            for slot in slot_range:
                @pl.when(held(place_of(kind, lax.rem(place_x + x_len - d, x_len), core), slot))
                def _(kind=kind, d=d, slot=slot):
                    go_x(kind, slot, d).wait_recv()
                    go_f(kind, slot, d).start()

    for slot in slot_range:
        @pl.when(held(own, slot))
        def _(slot=slot):
            stay(slot).wait()
            go_y(slot).wait_send()

        for kind in range(2):
            @pl.when(held(own if kind == 0 else far, slot))
            def _(kind=kind, slot=slot):
                for d in steps:
                    go_x(kind, slot, d).wait_send()
                go_c(kind, slot).wait_send()

            @pl.when(held(place_of(kind, place_x, 1 - core), slot))
            def _(kind=kind, slot=slot):
                go_c(kind, slot).wait_recv()

            for d in steps:
                from_x = lax.rem(place_x + x_len - d, x_len)

                @pl.when(held(place_of(kind, from_x, core), slot))
                def _(kind=kind, slot=slot, d=d):
                    go_f(kind, slot, d).wait_send()

                @pl.when(held(place_of(kind, from_x, 1 - core), slot))
                def _(kind=kind, slot=slot, d=d):
                    go_f(kind, slot, d).wait_recv()
    load.wait()

    rows = projected.shape[0]
    width = heads * HEAD

    def product(r):
        at = pl.ds(pl.multiple_of(r * rows, rows), rows)
        left = jnp.concatenate([merged[h, at, :] for h in range(heads)], axis=1)
        right = weight[pl.ds(pl.multiple_of(r * width, width), width), :]
        return jnp.dot(left, right, preferred_element_type=jnp.float32)

    projected[...] = product(0)

    @pl.loop(1, MERGE)
    def _(r):
        projected[...] += product(r)

    values = projected[...]
    lane = lax.broadcasted_iota(jnp.int32, (rows, LANES), 1)
    member = seg_ref[...] == lane
    squares = jnp.sum(values * values, axis=1, keepdims=True)
    tops = jnp.max(values, axis=1, keepdims=True)
    sums = jnp.sum(jnp.where(member, squares, 0.0), axis=0, keepdims=True)
    peaks = jnp.max(jnp.where(member, tops, masked_score), axis=0, keepdims=True)
    line = lax.broadcasted_iota(jnp.int32, (8, LANES), 0)

    def spread(stats, tile, me, count, target_of, send, recv):
        stats[me] = tile

        def send_to(d):
            return pltpu.make_async_remote_copy(
                src_ref=stats.at[me], dst_ref=stats.at[me],
                send_sem=send.at[d - 1], recv_sem=recv.at[d - 1],
                device_id=target_of(d), device_id_type=MESH,
            )

        for d in range(1, count):
            send_to(d).start()
        for d in range(1, count):
            send_to(d).wait()
        every = stats[...]
        return jnp.where(line == 0, jnp.sum(every, axis=0), jnp.max(every, axis=0))

    tile = jnp.where(line == 0, sums, peaks)
    tile = spread(part_stats, tile, part, tp, lambda d: (blk, lax.rem(part + d, tp)), p_send, p_recv)
    tile = spread(blk_stats, tile, blk, blks, lambda d: (lax.rem(blk + d, blks), part), b_send, b_recv)
    scale = lax.rsqrt(tile[0:1] / jnp.maximum(count_ref[...], 1.0) + epsilon)
    row_scale = jnp.sum(jnp.where(member, scale, 0.0), axis=1, keepdims=True)
    normed_ref[...] = (values * row_scale).astype(jnp.bfloat16)
    peak_ref[...] = jnp.broadcast_to(tile[1:2] * scale, (8, LANES))


def per_device(queries, keys, values, segment_ids, proj_weight):
    blks, tp = lax.axis_size("blk"), lax.axis_size("tp")
    blk = lax.axis_index("blk")
    rows, width = queries.shape
    heads = width // HEAD
    tokens = segment_ids.shape[0]
    block_len = tokens // blks
    pairs, places = blks // 2, 2 * tp
    slots = -(-heads // places)
    peers = places - 1
    pair_len = 2 * block_len
    columns = proj_weight.shape[1]
    dma, anywhere = pltpu.SemaphoreType.DMA, pl.BlockSpec(memory_space=pl.ANY)
    in_vmem = pl.BlockSpec(memory_space=pltpu.VMEM)

    begin = (blk // 2) * pair_len
    edge = jnp.full((block_len,), -2, jnp.int32)
    key_segs = lax.dynamic_slice_in_dim(jnp.concatenate([edge, segment_ids, edge]), begin, 2 * pair_len)
    query_segs = lax.dynamic_slice_in_dim(segment_ids, begin, pair_len)
    tiles = query_segs.reshape(pair_len // QUERY_TILE, QUERY_TILE)
    least = jnp.min(jnp.where(tiles >= 0, tiles, tokens), axis=1)[:, None]
    most = jnp.max(tiles, axis=1)[:, None]
    meets = (key_segs[None] >= least) & (key_segs[None] <= most)
    chunk = jnp.arange(2 * pair_len, dtype=jnp.int32)[None] // KEY_TILE
    low = jnp.min(jnp.where(meets, chunk, 2 * pair_len), axis=1)
    high = jnp.max(jnp.where(meets, chunk + 1, 0), axis=1)
    row_segs = lax.dynamic_slice_in_dim(segment_ids, blk * block_len, block_len)[::MERGE]
    lanes = jnp.arange(LANES, dtype=jnp.int32)
    counts = jnp.sum((segment_ids[::MERGE][:, None] == lanes).astype(jnp.float32), axis=0, keepdims=True)
    counts = counts * (columns * tp)

    held = slots * HEAD
    query_cols, key_cols, value_cols = pl.pallas_call(
        functools.partial(exchange_kernel, tp, pairs, heads, slots, block_len),
        out_shape=[
            jax.ShapeDtypeStruct((pair_len, held), jnp.bfloat16),
            jax.ShapeDtypeStruct((2 * pair_len, held), jnp.bfloat16),
            jax.ShapeDtypeStruct((2 * pair_len, held), jnp.bfloat16),
        ],
        in_specs=[anywhere] * 3,
        out_specs=[anywhere] * 3,
        scratch_shapes=[dma((3, peers)), dma((3, peers)), dma((2, 2)), dma((2, 2)), dma((3,))],
        compiler_params=pltpu.CompilerParams(collective_id=0, has_side_effects=True),
        name="exchange",
    )(queries, keys, values)

    per_block = block_len // QUERY_TILE
    merge_rows = QUERY_TILE // MERGE
    whole = lambda i, low, high: (0, 0)
    by_tile = lambda i, low, high: (i, 0)
    attended = pl.pallas_call(
        functools.partial(attend_kernel, slots),
        out_shape=jax.ShapeDtypeStruct((slots, 2, MERGE, block_len // MERGE, HEAD), jnp.bfloat16),
        grid_spec=pltpu.PrefetchScalarGridSpec(
            num_scalar_prefetch=2,
            grid=(2 * per_block,),
            in_specs=[
                pl.BlockSpec((QUERY_TILE, held), by_tile),
                pl.BlockSpec((2 * pair_len, held), whole),
                pl.BlockSpec((2 * pair_len, held), whole),
                pl.BlockSpec((QUERY_TILE, 1), by_tile),
                pl.BlockSpec((1, 2 * pair_len), whole),
            ],
            out_specs=pl.BlockSpec(
                (slots, 1, MERGE, merge_rows, HEAD),
                lambda i, low, high: (0, i // per_block, 0, i % per_block, 0),
            ),
            scratch_shapes=[pltpu.VMEM((slots, QUERY_TILE, HEAD), jnp.float32)],
        ),
        compiler_params=pltpu.CompilerParams(vmem_limit_bytes=40 * 1024 * 1024),
        name="attend",
    )(
        low, high, query_cols, key_cols, value_cols,
        jnp.where(query_segs >= 0, query_segs, -3)[:, None], key_segs[None],
    )
    attended = attended.reshape(slots, 2, block_len, HEAD)

    x_len = tp // 2
    merged_rows = block_len // MERGE
    sems = [dma(()), dma((slots,)), dma((slots,)), dma((slots,))]
    sems += [dma((2, slots, x_len - 1))] * 2 + [dma((2, slots))] * 2 + [dma((2, slots, x_len - 1))] * 2
    sems += [dma((tp - 1,))] * 2 + [dma((blks - 1,))] * 2
    normed, peaks = pl.pallas_call(
        functools.partial(project_kernel, tp, blks, heads, slots),
        out_shape=[
            jax.ShapeDtypeStruct((merged_rows, columns), jnp.bfloat16),
            jax.ShapeDtypeStruct((8, LANES), jnp.float32),
        ],
        in_specs=[in_vmem, anywhere, in_vmem, in_vmem],
        out_specs=[in_vmem, in_vmem],
        scratch_shapes=[
            pltpu.VMEM((heads, block_len, HEAD), jnp.bfloat16),
            pltpu.VMEM(proj_weight.shape, jnp.bfloat16),
            pltpu.VMEM((merged_rows, columns), jnp.float32),
            pltpu.VMEM((tp, 8, LANES), jnp.float32),
            pltpu.VMEM((blks, 8, LANES), jnp.float32),
        ] + sems,
        compiler_params=pltpu.CompilerParams(
            collective_id=1, has_side_effects=True, vmem_limit_bytes=48 * 1024 * 1024
        ),
        name="project",
    )(attended, proj_weight, row_segs[:, None], counts)
    return normed, peaks[0, :blks]


def solution(mesh):
    in_specs = (
        P(("blk", "tp"), None),
        P(("blk", "tp"), None),
        P(("blk", "tp"), None),
        P(),
        P(None, "tp"),
    )
    out_specs = (P("blk", "tp"), P())
    return jax.shard_map(
        per_device, mesh=mesh, in_specs=in_specs, out_specs=out_specs, check_vma=False
    )
```

```python
import functools

import jax
import jax.numpy as jnp
from jax import lax
from jax.experimental import pallas as pl
from jax.experimental.pallas import tpu as pltpu
from jax.sharding import PartitionSpec as P

HEAD = 128
MERGE = 4
QUERY_TILE = 256
KEY_TILE = 768
LANES = 128
masked_score = -1e30
least_top = -1e20
epsilon = 1e-06
score_scale = HEAD ** (-0.5) * 1.4426950408889634
MESH = pl.DeviceIdType.MESH


def start_head(place, places, heads):
    return (place * heads) // places


def whole_kernel(
    tp, blks, heads, slots, block_len,
    q_in, k_in, v_in, seg_ref, w_ref, normed_ref, peak_ref,
    queries, keys, values_held, key_marks, query_marks, o_ref, mixed_ref,
    merged, weight, projected, part_stats, blk_stats,
    send, recv, keep_sem, pass_send, pass_recv,
    w_sem, own_sem, y_send, y_recv, x_send, x_recv, c_send, c_recv, f_send, f_recv,
    p_send, p_recv, b_send, b_recv,
):
    blk, part = lax.axis_index("blk"), lax.axis_index("tp")
    side, place_x, core = lax.rem(blk, 2), part // 2, lax.rem(part, 2)
    pair, pairs = blk // 2, blks // 2
    x_len, places = tp // 2, 2 * tp
    place = side * tp + part
    sibling = (blk, part + 1 - 2 * core)
    across = (blk + 1 - 2 * side, part)
    slab = q_in.shape[0]
    load = pltpu.make_async_copy(w_ref, weight, w_sem)

    barrier = pltpu.get_barrier_semaphore()
    for d in range(1, tp):
        other_part = lax.rem(part + d, tp)
        pl.semaphore_signal(barrier, inc=1, device_id=(blk, other_part), device_id_type=MESH)
        pl.semaphore_signal(barrier, inc=1, device_id=(across[0], other_part), device_id_type=MESH)
    for d in range(1, blks):
        pl.semaphore_signal(barrier, inc=1, device_id=(lax.rem(blk + d, blks), part), device_id_type=MESH)

    has_prev, has_next = pair > 0, pair < pairs - 1

    @pl.when(pair == 0)
    def _():
        for ref in (keys, values_held):
            ref[:, 0:block_len, :] = jnp.zeros((slots, block_len, HEAD), jnp.bfloat16)

    @pl.when(pair == pairs - 1)
    def _():
        for ref in (keys, values_held):
            ref[:, 3 * block_len : 4 * block_len, :] = jnp.zeros((slots, block_len, HEAD), jnp.bfloat16)

    pl.semaphore_wait(barrier, 2 * (tp - 1) + blks - 1)

    def first(place):
        return start_head(place, places, heads)

    def held(place, slot):
        return slot < first(place + 1) - first(place)

    def place_of(kind, to_x, to_core):
        return (side if kind == 0 else 1 - side) * tp + to_x * 2 + to_core

    def copy(src, head, send_sem, recv_sem, target):
        return pltpu.make_async_remote_copy(
            src_ref=src, dst_ref=merged.at[head], send_sem=send_sem, recv_sem=recv_sem,
            device_id=target, device_id_type=MESH,
        )

    own = place_of(0, place_x, core)
    far = place_of(1, place_x, core)

    def clipped(place, slot):
        return jnp.minimum(first(place) + slot, heads - 1)

    def stay(slot):
        return pltpu.make_async_copy(o_ref.at[slot, side], merged.at[clipped(own, slot)], own_sem.at[slot])

    def go_y(slot):
        return copy(o_ref.at[slot, 1 - side], clipped(own, slot), y_send.at[slot], y_recv.at[slot], across)

    def source(kind, slot):
        return o_ref.at[slot, side] if kind == 0 else merged.at[clipped(far, slot)]

    def go_x(kind, slot, d):
        target = (blk, lax.rem(place_x + d, x_len) * 2 + core)
        head = clipped(own if kind == 0 else far, slot)
        return copy(source(kind, slot), head, x_send.at[kind, slot, d - 1], x_recv.at[kind, slot, d - 1], target)

    def go_c(kind, slot):
        head = clipped(own if kind == 0 else far, slot)
        return copy(source(kind, slot), head, c_send.at[kind, slot], c_recv.at[kind, slot], sibling)

    def go_f(kind, slot, d):
        came = clipped(place_of(kind, lax.rem(place_x + x_len - d, x_len), core), slot)
        return copy(merged.at[came], came, f_send.at[kind, slot, d - 1], f_recv.at[kind, slot, d - 1], sibling)

    offsets = [(dy, dt) for dy in (1, 0) for dt in range(tp) if (dy, dt) != (0, 0)]
    arrays = ((k_in, keys, block_len), (v_in, values_held, block_len), (q_in, queries, 0))

    def push(a, slot, i):
        src, dst, base = arrays[a]
        dy, dt = offsets[i]
        to_side, to_part = lax.rem(side + dy, 2), lax.rem(part + dt, tp)
        column = clipped(to_side * tp + to_part, slot) * HEAD
        return pltpu.make_async_remote_copy(
            src_ref=src.at[:, pl.ds(pl.multiple_of(column, HEAD), HEAD)],
            dst_ref=dst.at[slot, pl.ds(pl.multiple_of(base + place * slab, slab), slab), :],
            send_sem=send.at[a, slot, i],
            recv_sem=recv.at[a, slot, i],
            device_id=(pair * 2 + to_side, to_part),
            device_id_type=MESH,
        )

    def pushed_to(slot, i):
        dy, dt = offsets[i]
        return held(lax.rem(side + dy, 2) * tp + lax.rem(part + dt, tp), slot)

    def keep(a, slot):
        src, dst, base = arrays[a]
        return pltpu.make_async_copy(
            src.at[:, pl.ds(pl.multiple_of(clipped(place, slot) * HEAD, HEAD), HEAD)],
            dst.at[slot, pl.ds(pl.multiple_of(base + place * slab, slab), slab), :],
            keep_sem.at[a, slot],
        )

    def hand_on(a, slot, forward):
        dst = arrays[a][1]
        if forward:
            src_rows, dst_rows, target = pl.ds(2 * block_len, block_len), pl.ds(0, block_len), blk + 2
        else:
            src_rows, dst_rows, target = pl.ds(block_len, block_len), pl.ds(3 * block_len, block_len), blk - 2
        return pltpu.make_async_remote_copy(
            src_ref=dst.at[slot, src_rows, :],
            dst_ref=dst.at[slot, dst_rows, :],
            send_sem=pass_send.at[a, slot, forward],
            recv_sem=pass_recv.at[a, slot, forward],
            device_id=(target, part),
            device_id_type=MESH,
        )

    def start_all(a, slot):
        for i in range(len(offsets)):
            @pl.when(pushed_to(slot, i))
            def _(i=i):
                push(a, slot, i).start()

        @pl.when(held(own, slot))
        def _():
            keep(a, slot).start()

    def sent_all(a, slot):
        for i in range(len(offsets)):
            @pl.when(pushed_to(slot, i))
            def _(i=i):
                push(a, slot, i).wait_send()

    def arrive_all(a, slot):
        @pl.when(held(own, slot))
        def _():
            for i in range(len(offsets)):
                push(a, slot, i).wait_recv()
            keep(a, slot).wait()

    def hand_on_all(a, slot):
        @pl.when(held(own, slot) & has_prev)
        def _():
            hand_on(a, slot, 0).start()

        @pl.when(held(own, slot) & has_next)
        def _():
            hand_on(a, slot, 1).start()

    def handed_all(slot):
        for a in range(2):
            @pl.when(held(own, slot) & has_prev)
            def _(a=a):
                hand_on(a, slot, 1).wait_recv()

            @pl.when(held(own, slot) & has_next)
            def _(a=a):
                hand_on(a, slot, 0).wait_recv()

    def handed_away(slot):
        for a in range(2):
            @pl.when(held(own, slot) & has_prev)
            def _(a=a):
                hand_on(a, slot, 0).wait_send()

            @pl.when(held(own, slot) & has_next)
            def _(a=a):
                hand_on(a, slot, 1).wait_send()

    window = 2 * block_len + QUERY_TILE

    def attend(slot, block):
        per_block = block_len // QUERY_TILE
        part_rows = QUERY_TILE // MERGE

        @pl.loop(0, per_block)
        def _(n):
            begin = pl.multiple_of((block * per_block + n) * QUERY_TILE, QUERY_TILE)
            at = pl.ds(begin, QUERY_TILE)
            left = jnp.concatenate([queries[slot, at, :], query_marks[at, :]], axis=1)
            chunks = [pl.ds(pl.multiple_of(begin + c, QUERY_TILE), KEY_TILE) for c in range(0, window, KEY_TILE)]
            scores = [
                lax.dot_general(
                    left, jnp.concatenate([keys[slot, c, :], key_marks[c, :]], axis=1),
                    (((1,), (1,)), ((), ())), preferred_element_type=jnp.float32,
                )
                for c in chunks
            ]
            top = functools.reduce(jnp.maximum, [jnp.max(x, axis=1, keepdims=True) for x in scores])
            top = jnp.maximum(top, least_top)
            ones = jnp.ones((KEY_TILE, HEAD), jnp.bfloat16)
            mixed = jnp.zeros((QUERY_TILE, 2 * HEAD), jnp.float32)
            for x, c in zip(scores, chunks):
                terms = jnp.exp2((x - top) * score_scale).astype(jnp.bfloat16)
                right = jnp.concatenate([values_held[slot, c, :], ones], axis=1)
                mixed += jnp.dot(terms, right, preferred_element_type=jnp.float32)
            mixed_ref[...] = mixed[:, :HEAD] / jnp.maximum(mixed[:, HEAD:], 1.0)
            for r in range(MERGE):
                rows_to = pl.ds(pl.multiple_of(r * (block_len // MERGE) + n * part_rows, part_rows), part_rows)
                o_ref[slot, block, rows_to, :] = mixed_ref[
                    pl.ds(r, part_rows, stride=MERGE), :
                ].astype(jnp.bfloat16)

    slot_range, steps = range(slots), range(1, x_len)

    def send_own(slot):
        @pl.when(held(own, slot))
        def _():
            attend(slot, side)
            for d in steps:
                go_x(0, slot, d).start()
            go_c(0, slot).start()
            stay(slot).start()

    def send_far(slot):
        @pl.when(held(far, slot))
        def _():
            go_y(slot).wait_recv()
            for d in steps:
                go_x(1, slot, d).start()
            go_c(1, slot).start()

    def send_on(slot, kind):
        for d in steps:
            @pl.when(held(place_of(kind, lax.rem(place_x + x_len - d, x_len), core), slot))
            def _(d=d):
                go_x(kind, slot, d).wait_recv()
                go_f(kind, slot, d).start()

    for a in range(3):
        start_all(a, 0)
    load.start()

    lane_of_key = lax.broadcasted_iota(jnp.int32, (block_len, LANES), 1)
    for n in range(4):
        at = slice(n * block_len, (n + 1) * block_len)
        segs = seg_ref[at, :]
        marked = jnp.where(segs >= 0, segs, LANES - 1) == lane_of_key
        key_marks[at, :] = jnp.where(marked, 1.0, 0.0).astype(jnp.bfloat16)
        if n in (1, 2):
            query_marks[slice((n - 1) * block_len, n * block_len), :] = jnp.where(
                segs == lane_of_key, 0.0, masked_score
            ).astype(jnp.bfloat16)

    for slot in slot_range:
        for a in range(3):
            arrive_all(a, slot)
            if a < 2:
                hand_on_all(a, slot)
            if slot + 1 < slots:
                start_all(a, slot + 1)
        handed_all(slot)
        if slot > 0:
            send_far(slot - 1)

        @pl.when(held(own, slot))
        def _(slot=slot):
            attend(slot, 1 - side)
            go_y(slot).start()

        if slot > 0:
            for kind in range(2):
                send_on(slot - 1, kind)
        send_own(slot)
    send_far(slots - 1)
    for kind in range(2):
        send_on(slots - 1, kind)
    for slot in slot_range:
        for a in range(3):
            sent_all(a, slot)
        handed_away(slot)

    for slot in slot_range:
        @pl.when(held(own, slot))
        def _(slot=slot):
            stay(slot).wait()
            go_y(slot).wait_send()

        for kind in range(2):
            @pl.when(held(own if kind == 0 else far, slot))
            def _(kind=kind, slot=slot):
                for d in steps:
                    go_x(kind, slot, d).wait_send()
                go_c(kind, slot).wait_send()

            @pl.when(held(place_of(kind, place_x, 1 - core), slot))
            def _(kind=kind, slot=slot):
                go_c(kind, slot).wait_recv()

            for d in steps:
                from_x = lax.rem(place_x + x_len - d, x_len)

                @pl.when(held(place_of(kind, from_x, core), slot))
                def _(kind=kind, slot=slot, d=d):
                    go_f(kind, slot, d).wait_send()

                @pl.when(held(place_of(kind, from_x, 1 - core), slot))
                def _(kind=kind, slot=slot, d=d):
                    go_f(kind, slot, d).wait_recv()
    load.wait()

    rows = projected.shape[0]
    width = heads * HEAD

    def product(r):
        at = pl.ds(pl.multiple_of(r * rows, rows), rows)
        left = jnp.concatenate([merged[h, at, :] for h in range(heads)], axis=1)
        right = weight[pl.ds(pl.multiple_of(r * width, width), width), :]
        return jnp.dot(left, right, preferred_element_type=jnp.float32)

    projected[...] = product(0)

    @pl.loop(1, MERGE)
    def _(r):
        projected[...] += product(r)

    values = projected[...]
    lane = lax.broadcasted_iota(jnp.int32, (rows, LANES), 1)
    own_rows = pl.ds((1 + side) * block_len, rows, stride=MERGE)
    member = seg_ref[own_rows, :] == lane
    squares = jnp.sum(values * values, axis=1, keepdims=True)
    tops = jnp.max(values, axis=1, keepdims=True)
    sums = jnp.sum(jnp.where(member, squares, 0.0), axis=0, keepdims=True)
    peaks = jnp.max(jnp.where(member, tops, masked_score), axis=0, keepdims=True)
    counts = jnp.sum(member.astype(jnp.float32), axis=0, keepdims=True) * values.shape[1]
    line = lax.broadcasted_iota(jnp.int32, (8, LANES), 0)

    def spread(stats, tile, me, count, target_of, send, recv):
        stats[me] = tile

        def send_to(d):
            return pltpu.make_async_remote_copy(
                src_ref=stats.at[me], dst_ref=stats.at[me],
                send_sem=send.at[d - 1], recv_sem=recv.at[d - 1],
                device_id=target_of(d), device_id_type=MESH,
            )

        for d in range(1, count):
            send_to(d).start()
        for d in range(1, count):
            send_to(d).wait()
        every = stats[...]
        return jnp.where(line == 1, jnp.max(every, axis=0), jnp.sum(every, axis=0))

    tile = jnp.where(line == 0, sums, jnp.where(line == 1, peaks, counts))
    tile = spread(part_stats, tile, part, tp, lambda d: (blk, lax.rem(part + d, tp)), p_send, p_recv)
    tile = spread(blk_stats, tile, blk, blks, lambda d: (lax.rem(blk + d, blks), part), b_send, b_recv)
    scale = lax.rsqrt(tile[0:1] / jnp.maximum(tile[2:3], 1.0) + epsilon)
    row_scale = jnp.sum(jnp.where(member, scale, 0.0), axis=1, keepdims=True)
    normed_ref[...] = (values * row_scale).astype(jnp.bfloat16)
    peak_ref[...] = jnp.broadcast_to(tile[1:2] * scale, (8, LANES))


def per_device(queries, keys, values, segment_ids, proj_weight):
    blks, tp = lax.axis_size("blk"), lax.axis_size("tp")
    blk = lax.axis_index("blk")
    width = queries.shape[1]
    heads = width // HEAD
    block_len = segment_ids.shape[0] // blks
    places = 2 * tp
    slots = -(-heads // places)
    peers = places - 1
    pair_len = 2 * block_len
    columns = proj_weight.shape[1]
    dma, anywhere = pltpu.SemaphoreType.DMA, pl.BlockSpec(memory_space=pl.ANY)
    in_vmem = pl.BlockSpec(memory_space=pltpu.VMEM)
    edge = jnp.full((block_len,), -2, jnp.int32)
    pair_segs = lax.dynamic_slice_in_dim(
        jnp.concatenate([edge, segment_ids, edge]), (blk // 2) * pair_len, 2 * pair_len
    )
    x_len = tp // 2
    merged_rows = block_len // MERGE
    sems = [dma((3, slots, peers))] * 2 + [dma((3, slots))] + [dma((2, slots, 2))] * 2
    sems += [dma(()), dma((slots,)), dma((slots,)), dma((slots,))]
    sems += [dma((2, slots, x_len - 1))] * 2 + [dma((2, slots))] * 2 + [dma((2, slots, x_len - 1))] * 2
    sems += [dma((tp - 1,))] * 2 + [dma((blks - 1,))] * 2
    vmem16 = lambda *shape: pltpu.VMEM(shape, jnp.bfloat16)
    vmem32 = lambda *shape: pltpu.VMEM(shape, jnp.float32)
    normed, peaks = pl.pallas_call(
        functools.partial(whole_kernel, tp, blks, heads, slots, block_len),
        out_shape=[
            jax.ShapeDtypeStruct((merged_rows, columns), jnp.bfloat16),
            jax.ShapeDtypeStruct((8, LANES), jnp.float32),
        ],
        in_specs=[anywhere, anywhere, anywhere, in_vmem, anywhere],
        out_specs=[in_vmem, in_vmem],
        scratch_shapes=[
            vmem16(slots, pair_len, HEAD),
            vmem16(slots, 2 * pair_len, HEAD),
            vmem16(slots, 2 * pair_len, HEAD),
            vmem16(2 * pair_len, LANES),
            vmem16(pair_len, LANES),
            vmem16(slots, 2, block_len, HEAD),
            vmem32(QUERY_TILE, HEAD),
            vmem16(heads, block_len, HEAD),
            vmem16(*proj_weight.shape),
            vmem32(merged_rows, columns),
            vmem32(tp, 8, LANES),
            vmem32(blks, 8, LANES),
        ] + sems,
        compiler_params=pltpu.CompilerParams(
            collective_id=0, has_side_effects=True, vmem_limit_bytes=56 * 1024 * 1024
        ),
        name="whole",
    )(queries, keys, values, pair_segs[:, None], proj_weight)
    return normed, peaks[0, :blks]


def solution(mesh):
    in_specs = (
        P(("blk", "tp"), None),
        P(("blk", "tp"), None),
        P(("blk", "tp"), None),
        P(),
        P(None, "tp"),
    )
    out_specs = (P("blk", "tp"), P())
    return jax.shard_map(
        per_device, mesh=mesh, in_specs=in_specs, out_specs=out_specs, check_vma=False
    )
```

```python
import functools

import jax
import jax.numpy as jnp
from jax import lax
from jax.experimental import pallas as pl
from jax.experimental.pallas import tpu as pltpu
from jax.sharding import PartitionSpec as P

HEAD = 128
MERGE = 4
QUERY_TILE = 256
KEY_TILE = 768
TOGETHER = 2
LANES = 128
masked_score = -1e30
least_top = -1e20
epsilon = 1e-06
score_scale = HEAD ** (-0.5) * 1.4426950408889634
MESH = pl.DeviceIdType.MESH


def start_head(place, places, heads):
    return (place * heads) // places


def whole_kernel(
    tp, blks, heads, slots, block_len,
    q_in, k_in, v_in, seg_ref, w_ref, normed_ref, peak_ref,
    queries, keys, values_held, key_marks, query_marks, row_marks, o_ref, mixed_ref,
    merged, weight, projected, part_stats, blk_stats,
    send, recv, keep_sem, pass_send, pass_recv,
    w_sem, own_sem, y_send, y_recv, x_send, x_recv, c_send, c_recv, f_send, f_recv,
    p_send, p_recv, b_send, b_recv,
):
    blk, part = lax.axis_index("blk"), lax.axis_index("tp")
    side, place_x, core = lax.rem(blk, 2), part // 2, lax.rem(part, 2)
    pair, pairs = blk // 2, blks // 2
    x_len, places = tp // 2, 2 * tp
    place = side * tp + part
    sibling = (blk, part + 1 - 2 * core)
    across = (blk + 1 - 2 * side, part)
    slab = q_in.shape[0]
    load = pltpu.make_async_copy(w_ref, weight, w_sem)

    barrier = pltpu.get_barrier_semaphore()
    for d in range(1, tp):
        other_part = lax.rem(part + d, tp)
        pl.semaphore_signal(barrier, inc=1, device_id=(blk, other_part), device_id_type=MESH)
        pl.semaphore_signal(barrier, inc=1, device_id=(across[0], other_part), device_id_type=MESH)
    for d in range(1, blks):
        pl.semaphore_signal(barrier, inc=1, device_id=(lax.rem(blk + d, blks), part), device_id_type=MESH)

    has_prev, has_next = pair > 0, pair < pairs - 1

    @pl.when(pair == 0)
    def _():
        for ref in (keys, values_held):
            ref[:, 0:block_len, :] = jnp.zeros((slots, block_len, HEAD), jnp.bfloat16)

    @pl.when(pair == pairs - 1)
    def _():
        for ref in (keys, values_held):
            ref[:, 3 * block_len : 4 * block_len, :] = jnp.zeros((slots, block_len, HEAD), jnp.bfloat16)

    pl.semaphore_wait(barrier, 2 * (tp - 1) + blks - 1)

    def first(place):
        return start_head(place, places, heads)

    def held(place, slot):
        return slot < first(place + 1) - first(place)

    def place_of(kind, to_x, to_core):
        return (side if kind == 0 else 1 - side) * tp + to_x * 2 + to_core

    def copy(src, head, send_sem, recv_sem, target):
        return pltpu.make_async_remote_copy(
            src_ref=src, dst_ref=merged.at[head], send_sem=send_sem, recv_sem=recv_sem,
            device_id=target, device_id_type=MESH,
        )

    own = place_of(0, place_x, core)
    far = place_of(1, place_x, core)

    def clipped(place, slot):
        return jnp.minimum(first(place) + slot, heads - 1)

    def stay(slot):
        return pltpu.make_async_copy(o_ref.at[slot, side], merged.at[clipped(own, slot)], own_sem.at[slot])

    def go_y(slot):
        return copy(o_ref.at[slot, 1 - side], clipped(own, slot), y_send.at[slot], y_recv.at[slot], across)

    def source(kind, slot):
        return o_ref.at[slot, side] if kind == 0 else merged.at[clipped(far, slot)]

    def go_x(kind, slot, d):
        target = (blk, lax.rem(place_x + d, x_len) * 2 + core)
        head = clipped(own if kind == 0 else far, slot)
        return copy(source(kind, slot), head, x_send.at[kind, slot, d - 1], x_recv.at[kind, slot, d - 1], target)

    def go_c(kind, slot):
        head = clipped(own if kind == 0 else far, slot)
        return copy(source(kind, slot), head, c_send.at[kind, slot], c_recv.at[kind, slot], sibling)

    def go_f(kind, slot, d):
        came = clipped(place_of(kind, lax.rem(place_x + x_len - d, x_len), core), slot)
        return copy(merged.at[came], came, f_send.at[kind, slot, d - 1], f_recv.at[kind, slot, d - 1], sibling)

    offsets = [(dy, dt) for dy in (1, 0) for dt in range(tp) if (dy, dt) != (0, 0)]
    arrays = ((k_in, keys, block_len), (v_in, values_held, block_len), (q_in, queries, 0))

    def push(a, slot, i):
        src, dst, base = arrays[a]
        dy, dt = offsets[i]
        to_side, to_part = lax.rem(side + dy, 2), lax.rem(part + dt, tp)
        column = clipped(to_side * tp + to_part, slot) * HEAD
        return pltpu.make_async_remote_copy(
            src_ref=src.at[:, pl.ds(pl.multiple_of(column, HEAD), HEAD)],
            dst_ref=dst.at[slot, pl.ds(pl.multiple_of(base + place * slab, slab), slab), :],
            send_sem=send.at[a, slot, i],
            recv_sem=recv.at[a, slot, i],
            device_id=(pair * 2 + to_side, to_part),
            device_id_type=MESH,
        )

    def pushed_to(slot, i):
        dy, dt = offsets[i]
        return held(lax.rem(side + dy, 2) * tp + lax.rem(part + dt, tp), slot)

    def keep(a, slot):
        src, dst, base = arrays[a]
        return pltpu.make_async_copy(
            src.at[:, pl.ds(pl.multiple_of(clipped(place, slot) * HEAD, HEAD), HEAD)],
            dst.at[slot, pl.ds(pl.multiple_of(base + place * slab, slab), slab), :],
            keep_sem.at[a, slot],
        )

    def hand_on(a, slot, forward):
        dst = arrays[a][1]
        if forward:
            src_rows, dst_rows, target = pl.ds(2 * block_len, block_len), pl.ds(0, block_len), blk + 2
        else:
            src_rows, dst_rows, target = pl.ds(block_len, block_len), pl.ds(3 * block_len, block_len), blk - 2
        return pltpu.make_async_remote_copy(
            src_ref=dst.at[slot, src_rows, :],
            dst_ref=dst.at[slot, dst_rows, :],
            send_sem=pass_send.at[a, slot, forward],
            recv_sem=pass_recv.at[a, slot, forward],
            device_id=(target, part),
            device_id_type=MESH,
        )

    def start_all(a, slot):
        for i in range(len(offsets)):
            @pl.when(pushed_to(slot, i))
            def _(i=i):
                push(a, slot, i).start()

        @pl.when(held(own, slot))
        def _():
            keep(a, slot).start()

    def sent_all(a, slot):
        for i in range(len(offsets)):
            @pl.when(pushed_to(slot, i))
            def _(i=i):
                push(a, slot, i).wait_send()

    def arrive_all(a, slot):
        @pl.when(held(own, slot))
        def _():
            for i in range(len(offsets)):
                push(a, slot, i).wait_recv()
            keep(a, slot).wait()

    def hand_on_all(a, slot):
        @pl.when(held(own, slot) & has_prev)
        def _():
            hand_on(a, slot, 0).start()

        @pl.when(held(own, slot) & has_next)
        def _():
            hand_on(a, slot, 1).start()

    def handed_all(slot):
        for a in range(2):
            @pl.when(held(own, slot) & has_prev)
            def _(a=a):
                hand_on(a, slot, 1).wait_recv()

            @pl.when(held(own, slot) & has_next)
            def _(a=a):
                hand_on(a, slot, 0).wait_recv()

    def handed_away(slot):
        for a in range(2):
            @pl.when(held(own, slot) & has_prev)
            def _(a=a):
                hand_on(a, slot, 0).wait_send()

            @pl.when(held(own, slot) & has_next)
            def _(a=a):
                hand_on(a, slot, 1).wait_send()

    window = 2 * block_len + QUERY_TILE

    def attend(slot, block):
        per_block = block_len // QUERY_TILE
        part_rows = QUERY_TILE // MERGE

        @pl.loop(0, per_block // TOGETHER)
        def _(step):
            tiles = [step * TOGETHER + u for u in range(TOGETHER)]
            at, chunks, scores = [], [], []
            for n in tiles:
                begin = pl.multiple_of((block * per_block + n) * QUERY_TILE, QUERY_TILE)
                rows = pl.ds(begin, QUERY_TILE)
                left = jnp.concatenate([queries[slot, rows, :], query_marks[rows, :]], axis=1)
                mine = [pl.ds(pl.multiple_of(begin + c, QUERY_TILE), KEY_TILE) for c in range(0, window, KEY_TILE)]
                chunks.append(mine)
                scores.append([
                    lax.dot_general(
                        left, jnp.concatenate([keys[slot, c, :], key_marks[c, :]], axis=1),
                        (((1,), (1,)), ((), ())), preferred_element_type=jnp.float32,
                    )
                    for c in mine
                ])
            ones = jnp.ones((KEY_TILE, HEAD), jnp.bfloat16)
            for u, n in enumerate(tiles):
                top = functools.reduce(jnp.maximum, [jnp.max(x, axis=1, keepdims=True) for x in scores[u]])
                top = jnp.maximum(top, least_top)
                mixed = jnp.zeros((QUERY_TILE, 2 * HEAD), jnp.float32)
                for x, c in zip(scores[u], chunks[u]):
                    terms = jnp.exp2((x - top) * score_scale).astype(jnp.bfloat16)
                    right = jnp.concatenate([values_held[slot, c, :], ones], axis=1)
                    mixed += jnp.dot(terms, right, preferred_element_type=jnp.float32)
                mixed_ref[u] = mixed[:, :HEAD] / jnp.maximum(mixed[:, HEAD:], 1.0)
            for u, n in enumerate(tiles):
                for r in range(MERGE):
                    rows_to = pl.ds(pl.multiple_of(r * (block_len // MERGE) + n * part_rows, part_rows), part_rows)
                    o_ref[slot, block, rows_to, :] = mixed_ref[
                        u, pl.ds(r, part_rows, stride=MERGE), :
                    ].astype(jnp.bfloat16)

    slot_range, steps = range(slots), range(1, x_len)

    def send_own(slot):
        @pl.when(held(own, slot))
        def _():
            attend(slot, side)
            for d in steps:
                go_x(0, slot, d).start()
            go_c(0, slot).start()
            stay(slot).start()

    def send_far(slot):
        @pl.when(held(far, slot))
        def _():
            go_y(slot).wait_recv()
            for d in steps:
                go_x(1, slot, d).start()
            go_c(1, slot).start()

    def send_on(slot, kind):
        for d in steps:
            @pl.when(held(place_of(kind, lax.rem(place_x + x_len - d, x_len), core), slot))
            def _(d=d):
                go_x(kind, slot, d).wait_recv()
                go_f(kind, slot, d).start()

    for a in range(3):
        start_all(a, 0)
    load.start()

    image = lax.broadcasted_iota(jnp.int32, (LANES, block_len), 0)
    lane = lax.broadcasted_iota(jnp.int32, (block_len, LANES), 1)
    for n in range(4):
        block = pair * 2 - 1 + n
        inside = (block >= 0) & (block < blks)
        from_row = jnp.clip(block, 0, blks - 1) * block_len
        segs = seg_ref[:, pl.ds(pl.multiple_of(from_row, LANES), block_len)]
        segs = jnp.where(inside & (segs >= 0), segs, LANES - 1)
        marks = jnp.where(segs == image, 1.0, 0.0).T
        key_marks[n * block_len : (n + 1) * block_len, :] = marks.astype(jnp.bfloat16)
        if n in (1, 2):
            query_marks[(n - 1) * block_len : n * block_len, :] = jnp.where(
                (marks > 0.5) & (lane < LANES - 1), 0.0, masked_score
            ).astype(jnp.bfloat16)
            row_marks[n - 1] = marks
    projected[...] = jnp.zeros_like(projected)

    for slot in slot_range:
        for a in range(3):
            arrive_all(a, slot)
            if a < 2:
                hand_on_all(a, slot)
            if slot + 1 < slots:
                start_all(a, slot + 1)
        handed_all(slot)
        if slot > 0:
            send_far(slot - 1)

        @pl.when(held(own, slot))
        def _(slot=slot):
            attend(slot, 1 - side)
            go_y(slot).start()

        if slot > 0:
            for kind in range(2):
                send_on(slot - 1, kind)
        send_own(slot)
    def gathered(slot):
        @pl.when(held(own, slot))
        def _():
            stay(slot).wait()

        for kind in range(2):
            @pl.when(held(place_of(kind, place_x, 1 - core), slot))
            def _(kind=kind):
                go_c(kind, slot).wait_recv()

            for d in steps:
                from_x = lax.rem(place_x + x_len - d, x_len)

                @pl.when(held(place_of(kind, from_x, 1 - core), slot))
                def _(kind=kind, d=d):
                    go_f(kind, slot, d).wait_recv()

    def let_go(slot):
        @pl.when(held(own, slot))
        def _():
            go_y(slot).wait_send()

        for kind in range(2):
            @pl.when(held(own if kind == 0 else far, slot))
            def _(kind=kind):
                for d in steps:
                    go_x(kind, slot, d).wait_send()
                go_c(kind, slot).wait_send()

            for d in steps:
                @pl.when(held(place_of(kind, lax.rem(place_x + x_len - d, x_len), core), slot))
                def _(kind=kind, d=d):
                    go_f(kind, slot, d).wait_send()

    rows = projected.shape[0]
    width = heads * HEAD

    def product(slot):
        present = [
            start_head(g, places, heads) + slot
            for g in range(places)
            if slot < start_head(g + 1, places, heads) - start_head(g, places, heads)
        ]

        @pl.loop(0, MERGE)
        def _(r):
            at = pl.ds(pl.multiple_of(r * rows, rows), rows)
            left = jnp.concatenate([merged[h, at, :] for h in present], axis=1)
            right = jnp.concatenate(
                [weight[pl.ds(pl.multiple_of(r * width + h * HEAD, HEAD), HEAD), :] for h in present], axis=0
            )
            projected[...] += jnp.dot(left, right, preferred_element_type=jnp.float32)

    send_far(slots - 1)
    load.wait()
    for slot in range(slots - 1):
        gathered(slot)
        product(slot)
    for kind in range(2):
        send_on(slots - 1, kind)
    gathered(slots - 1)
    product(slots - 1)
    for slot in slot_range:
        for a in range(3):
            sent_all(a, slot)
        handed_away(slot)
        let_go(slot)

    values = projected[...]
    lane = lax.broadcasted_iota(jnp.int32, (rows, LANES), 1)
    member = (row_marks[side, pl.ds(0, rows, stride=MERGE), :] > 0.5) & (lane < LANES - 1)
    squares = jnp.sum(values * values, axis=1, keepdims=True)
    tops = jnp.max(values, axis=1, keepdims=True)
    sums = jnp.sum(jnp.where(member, squares, 0.0), axis=0, keepdims=True)
    peaks = jnp.max(jnp.where(member, tops, masked_score), axis=0, keepdims=True)
    counts = jnp.sum(member.astype(jnp.float32), axis=0, keepdims=True) * values.shape[1]
    line = lax.broadcasted_iota(jnp.int32, (8, LANES), 0)

    def spread(stats, tile, me, count, target_of, send, recv):
        stats[me] = tile

        def send_to(d):
            return pltpu.make_async_remote_copy(
                src_ref=stats.at[me], dst_ref=stats.at[me],
                send_sem=send.at[d - 1], recv_sem=recv.at[d - 1],
                device_id=target_of(d), device_id_type=MESH,
            )

        for d in range(1, count):
            send_to(d).start()
        for d in range(1, count):
            send_to(d).wait()
        every = stats[...]
        return jnp.where(line == 1, jnp.max(every, axis=0), jnp.sum(every, axis=0))

    tile = jnp.where(line == 0, sums, jnp.where(line == 1, peaks, counts))
    tile = spread(part_stats, tile, part, tp, lambda d: (blk, lax.rem(part + d, tp)), p_send, p_recv)
    tile = spread(blk_stats, tile, blk, blks, lambda d: (lax.rem(blk + d, blks), part), b_send, b_recv)
    scale = lax.rsqrt(tile[0:1] / jnp.maximum(tile[2:3], 1.0) + epsilon)
    row_scale = jnp.sum(jnp.where(member, scale, 0.0), axis=1, keepdims=True)
    normed_ref[...] = (values * row_scale).astype(jnp.bfloat16)
    peak_ref[...] = (tile[1:2] * scale)[0, :blks]


def per_device(queries, keys, values, segment_ids, proj_weight):
    blks, tp = lax.axis_size("blk"), lax.axis_size("tp")
    width = queries.shape[1]
    heads = width // HEAD
    block_len = segment_ids.shape[0] // blks
    places = 2 * tp
    slots = -(-heads // places)
    peers = places - 1
    pair_len = 2 * block_len
    columns = proj_weight.shape[1]
    dma, anywhere = pltpu.SemaphoreType.DMA, pl.BlockSpec(memory_space=pl.ANY)
    in_vmem = pl.BlockSpec(memory_space=pltpu.VMEM)
    x_len = tp // 2
    merged_rows = block_len // MERGE
    sems = [dma((3, slots, peers))] * 2 + [dma((3, slots))] + [dma((2, slots, 2))] * 2
    sems += [dma(()), dma((slots,)), dma((slots,)), dma((slots,))]
    sems += [dma((2, slots, x_len - 1))] * 2 + [dma((2, slots))] * 2 + [dma((2, slots, x_len - 1))] * 2
    sems += [dma((tp - 1,))] * 2 + [dma((blks - 1,))] * 2
    vmem16 = lambda *shape: pltpu.VMEM(shape, jnp.bfloat16)
    vmem32 = lambda *shape: pltpu.VMEM(shape, jnp.float32)
    normed, peaks = pl.pallas_call(
        functools.partial(whole_kernel, tp, blks, heads, slots, block_len),
        out_shape=[
            jax.ShapeDtypeStruct((merged_rows, columns), jnp.bfloat16),
            jax.ShapeDtypeStruct((blks,), jnp.float32),
        ],
        in_specs=[anywhere, anywhere, anywhere, in_vmem, anywhere],
        out_specs=[in_vmem, in_vmem],
        scratch_shapes=[
            vmem16(slots, pair_len, HEAD),
            vmem16(slots, 2 * pair_len, HEAD),
            vmem16(slots, 2 * pair_len, HEAD),
            vmem16(2 * pair_len, LANES),
            vmem16(pair_len, LANES),
            vmem32(2, block_len, LANES),
            vmem16(slots, 2, block_len, HEAD),
            vmem32(TOGETHER, QUERY_TILE, HEAD),
            vmem16(heads, block_len, HEAD),
            vmem16(*proj_weight.shape),
            vmem32(merged_rows, columns),
            vmem32(tp, 8, LANES),
            vmem32(blks, 8, LANES),
        ] + sems,
        compiler_params=pltpu.CompilerParams(
            collective_id=0, has_side_effects=True, vmem_limit_bytes=56 * 1024 * 1024
        ),
        name="whole",
    )(queries, keys, values, segment_ids[None], proj_weight)
    return normed, peaks


def solution(mesh):
    in_specs = (
        P(("blk", "tp"), None),
        P(("blk", "tp"), None),
        P(("blk", "tp"), None),
        P(),
        P(None, "tp"),
    )
    out_specs = (P("blk", "tp"), P())
    return jax.shard_map(
        per_device, mesh=mesh, in_specs=in_specs, out_specs=out_specs, check_vma=False
    )
```

```python
import functools

import jax
import jax.numpy as jnp
from jax import lax
from jax.experimental import pallas as pl
from jax.experimental.pallas import tpu as pltpu
from jax.sharding import PartitionSpec as P

HEAD = 128
MERGE = 4
QUERY_TILE = 256
KEY_TILE = 768
TOGETHER = 4
LANES = 128
masked_score = -1e30
least_top = -1e20
epsilon = 1e-06
score_scale = HEAD ** (-0.5) * 1.4426950408889634
MESH = pl.DeviceIdType.MESH


def start_head(place, places, heads):
    return (place * heads) // places


def whole_kernel(
    tp, blks, heads, slots, block_len,
    q_in, k_in, v_in, seg_ref, w_ref, normed_ref, peak_ref,
    queries, keys, values_held, key_marks, query_marks, row_marks, o_ref, mixed_ref,
    merged, weight, projected, part_stats, blk_stats,
    send, recv, keep_sem, pass_send, pass_recv,
    w_sem, own_sem, y_send, y_recv, x_send, x_recv, c_send, c_recv, f_send, f_recv,
    p_send, p_recv, b_send, b_recv,
):
    blk, part = lax.axis_index("blk"), lax.axis_index("tp")
    side, place_x, core = lax.rem(blk, 2), part // 2, lax.rem(part, 2)
    pair, pairs = blk // 2, blks // 2
    x_len, places = tp // 2, 2 * tp
    place = side * tp + part
    sibling = (blk, part + 1 - 2 * core)
    across = (blk + 1 - 2 * side, part)
    slab = q_in.shape[0]
    load = pltpu.make_async_copy(w_ref, weight, w_sem)

    barrier = pltpu.get_barrier_semaphore()
    for d in range(1, tp):
        other_part = lax.rem(part + d, tp)
        pl.semaphore_signal(barrier, inc=1, device_id=(blk, other_part), device_id_type=MESH)
        pl.semaphore_signal(barrier, inc=1, device_id=(across[0], other_part), device_id_type=MESH)
    for d in range(1, blks):
        pl.semaphore_signal(barrier, inc=1, device_id=(lax.rem(blk + d, blks), part), device_id_type=MESH)

    has_prev, has_next = pair > 0, pair < pairs - 1

    @pl.when(pair == 0)
    def _():
        for ref in (keys, values_held):
            ref[:, 0:block_len, :] = jnp.zeros((slots, block_len, HEAD), jnp.bfloat16)

    @pl.when(pair == pairs - 1)
    def _():
        for ref in (keys, values_held):
            ref[:, 3 * block_len : 4 * block_len, :] = jnp.zeros((slots, block_len, HEAD), jnp.bfloat16)

    pl.semaphore_wait(barrier, 2 * (tp - 1) + blks - 1)

    def first(place):
        return start_head(place, places, heads)

    def held(place, slot):
        return slot < first(place + 1) - first(place)

    def place_of(kind, to_x, to_core):
        return (side if kind == 0 else 1 - side) * tp + to_x * 2 + to_core

    def copy(src, head, send_sem, recv_sem, target):
        return pltpu.make_async_remote_copy(
            src_ref=src, dst_ref=merged.at[head], send_sem=send_sem, recv_sem=recv_sem,
            device_id=target, device_id_type=MESH,
        )

    own = place_of(0, place_x, core)
    far = place_of(1, place_x, core)

    def clipped(place, slot):
        return jnp.minimum(first(place) + slot, heads - 1)

    def stay(slot):
        return pltpu.make_async_copy(o_ref.at[slot, side], merged.at[clipped(own, slot)], own_sem.at[slot])

    def go_y(slot):
        return copy(o_ref.at[slot, 1 - side], clipped(own, slot), y_send.at[slot], y_recv.at[slot], across)

    def source(kind, slot):
        return o_ref.at[slot, side] if kind == 0 else merged.at[clipped(far, slot)]

    def go_x(kind, slot, d):
        target = (blk, lax.rem(place_x + d, x_len) * 2 + core)
        head = clipped(own if kind == 0 else far, slot)
        return copy(source(kind, slot), head, x_send.at[kind, slot, d - 1], x_recv.at[kind, slot, d - 1], target)

    def go_c(kind, slot):
        head = clipped(own if kind == 0 else far, slot)
        return copy(source(kind, slot), head, c_send.at[kind, slot], c_recv.at[kind, slot], sibling)

    def go_f(kind, slot, d):
        came = clipped(place_of(kind, lax.rem(place_x + x_len - d, x_len), core), slot)
        return copy(merged.at[came], came, f_send.at[kind, slot, d - 1], f_recv.at[kind, slot, d - 1], sibling)

    offsets = [(dy, dt) for dy in (1, 0) for dt in range(tp) if (dy, dt) != (0, 0)]
    arrays = ((k_in, keys, block_len), (v_in, values_held, block_len), (q_in, queries, 0))

    def push(a, slot, i):
        src, dst, base = arrays[a]
        dy, dt = offsets[i]
        to_side, to_part = lax.rem(side + dy, 2), lax.rem(part + dt, tp)
        column = clipped(to_side * tp + to_part, slot) * HEAD
        return pltpu.make_async_remote_copy(
            src_ref=src.at[:, pl.ds(pl.multiple_of(column, HEAD), HEAD)],
            dst_ref=dst.at[slot, pl.ds(pl.multiple_of(base + place * slab, slab), slab), :],
            send_sem=send.at[a, slot, i],
            recv_sem=recv.at[a, slot, i],
            device_id=(pair * 2 + to_side, to_part),
            device_id_type=MESH,
        )

    def pushed_to(slot, i):
        dy, dt = offsets[i]
        return held(lax.rem(side + dy, 2) * tp + lax.rem(part + dt, tp), slot)

    def keep(a, slot):
        src, dst, base = arrays[a]
        return pltpu.make_async_copy(
            src.at[:, pl.ds(pl.multiple_of(clipped(place, slot) * HEAD, HEAD), HEAD)],
            dst.at[slot, pl.ds(pl.multiple_of(base + place * slab, slab), slab), :],
            keep_sem.at[a, slot],
        )

    def hand_on(a, slot, forward):
        dst = arrays[a][1]
        if forward:
            src_rows, dst_rows, target = pl.ds(2 * block_len, block_len), pl.ds(0, block_len), blk + 2
        else:
            src_rows, dst_rows, target = pl.ds(block_len, block_len), pl.ds(3 * block_len, block_len), blk - 2
        return pltpu.make_async_remote_copy(
            src_ref=dst.at[slot, src_rows, :],
            dst_ref=dst.at[slot, dst_rows, :],
            send_sem=pass_send.at[a, slot, forward],
            recv_sem=pass_recv.at[a, slot, forward],
            device_id=(target, part),
            device_id_type=MESH,
        )

    def start_all(a, slot):
        for i in range(len(offsets)):
            @pl.when(pushed_to(slot, i))
            def _(i=i):
                push(a, slot, i).start()

        @pl.when(held(own, slot))
        def _():
            keep(a, slot).start()

    def sent_all(a, slot):
        for i in range(len(offsets)):
            @pl.when(pushed_to(slot, i))
            def _(i=i):
                push(a, slot, i).wait_send()

    def arrive_all(a, slot):
        @pl.when(held(own, slot))
        def _():
            for i in range(len(offsets)):
                push(a, slot, i).wait_recv()
            keep(a, slot).wait()

    def hand_on_all(a, slot):
        @pl.when(held(own, slot) & has_prev)
        def _():
            hand_on(a, slot, 0).start()

        @pl.when(held(own, slot) & has_next)
        def _():
            hand_on(a, slot, 1).start()

    def handed_all(slot):
        for a in range(2):
            @pl.when(held(own, slot) & has_prev)
            def _(a=a):
                hand_on(a, slot, 1).wait_recv()

            @pl.when(held(own, slot) & has_next)
            def _(a=a):
                hand_on(a, slot, 0).wait_recv()

    def handed_away(slot):
        for a in range(2):
            @pl.when(held(own, slot) & has_prev)
            def _(a=a):
                hand_on(a, slot, 0).wait_send()

            @pl.when(held(own, slot) & has_next)
            def _(a=a):
                hand_on(a, slot, 1).wait_send()

    window = 2 * block_len + QUERY_TILE

    def attend(slot, block):
        per_block = block_len // QUERY_TILE
        part_rows = QUERY_TILE // MERGE

        @pl.loop(0, per_block // TOGETHER)
        def _(step):
            tiles = [step * TOGETHER + u for u in range(TOGETHER)]
            ones = jnp.ones((KEY_TILE, HEAD), jnp.bfloat16)

            def parts_of(n):
                begin = pl.multiple_of((block * per_block + n) * QUERY_TILE, QUERY_TILE)
                return begin, [
                    pl.ds(pl.multiple_of(begin + c, QUERY_TILE), KEY_TILE) for c in range(0, window, KEY_TILE)
                ]

            def score(n):
                begin, chunks = parts_of(n)
                rows = pl.ds(begin, QUERY_TILE)
                left = jnp.concatenate([queries[slot, rows, :], query_marks[rows, :]], axis=1)
                return [
                    lax.dot_general(
                        left, jnp.concatenate([keys[slot, c, :], key_marks[c, :]], axis=1),
                        (((1,), (1,)), ((), ())), preferred_element_type=jnp.float32,
                    )
                    for c in chunks
                ]

            def mix(u, n, scores):
                top = functools.reduce(jnp.maximum, [jnp.max(x, axis=1, keepdims=True) for x in scores])
                top = jnp.maximum(top, least_top)
                mixed = jnp.zeros((QUERY_TILE, 2 * HEAD), jnp.float32)
                for x, c in zip(scores, parts_of(n)[1]):
                    terms = jnp.exp2((x - top) * score_scale).astype(jnp.bfloat16)
                    right = jnp.concatenate([values_held[slot, c, :], ones], axis=1)
                    mixed += jnp.dot(terms, right, preferred_element_type=jnp.float32)
                mixed_ref[u] = mixed[:, :HEAD] / jnp.maximum(mixed[:, HEAD:], 1.0)

            ahead = score(tiles[0])
            for u, n in enumerate(tiles):
                scores = ahead
                if u + 1 < TOGETHER:
                    ahead = score(tiles[u + 1])
                mix(u, n, scores)
            for u, n in enumerate(tiles):
                for r in range(MERGE):
                    rows_to = pl.ds(pl.multiple_of(r * (block_len // MERGE) + n * part_rows, part_rows), part_rows)
                    o_ref[slot, block, rows_to, :] = mixed_ref[
                        u, pl.ds(r, part_rows, stride=MERGE), :
                    ].astype(jnp.bfloat16)

    slot_range, steps = range(slots), range(1, x_len)

    def send_own(slot):
        @pl.when(held(own, slot))
        def _():
            attend(slot, side)
            for d in steps:
                go_x(0, slot, d).start()
            go_c(0, slot).start()
            stay(slot).start()

    def send_far(slot):
        @pl.when(held(far, slot))
        def _():
            go_y(slot).wait_recv()
            for d in steps:
                go_x(1, slot, d).start()
            go_c(1, slot).start()

    def send_on(slot, kind):
        for d in steps:
            @pl.when(held(place_of(kind, lax.rem(place_x + x_len - d, x_len), core), slot))
            def _(d=d):
                go_x(kind, slot, d).wait_recv()
                go_f(kind, slot, d).start()

    start_all(0, 0)
    start_all(1, 0)
    load.start()

    image = lax.broadcasted_iota(jnp.int32, (LANES, block_len), 0)
    lane = lax.broadcasted_iota(jnp.int32, (block_len, LANES), 1)
    for n in range(4):
        block = pair * 2 - 1 + n
        inside = (block >= 0) & (block < blks)
        from_row = jnp.clip(block, 0, blks - 1) * block_len
        segs = seg_ref[:, pl.ds(pl.multiple_of(from_row, LANES), block_len)]
        segs = jnp.where(inside & (segs >= 0), segs, LANES - 1)
        marks = jnp.where(segs == image, 1.0, 0.0).T
        key_marks[n * block_len : (n + 1) * block_len, :] = marks.astype(jnp.bfloat16)
        if n in (1, 2):
            query_marks[(n - 1) * block_len : n * block_len, :] = jnp.where(
                (marks > 0.5) & (lane < LANES - 1), 0.0, masked_score
            ).astype(jnp.bfloat16)
            row_marks[n - 1] = marks
    projected[...] = jnp.zeros_like(projected)

    def arrive_and_hand_on(a, slot):
        arrive_all(a, slot)
        hand_on_all(a, slot)

    arrive_and_hand_on(0, 0)
    start_all(2, 0)
    arrive_and_hand_on(1, 0)
    for slot in slot_range:
        more = slot + 1 < slots
        if more:
            start_all(0, slot + 1)
            start_all(1, slot + 1)
        arrive_all(2, slot)
        if more:
            start_all(2, slot + 1)
        handed_all(slot)
        if more:
            arrive_and_hand_on(0, slot + 1)

        @pl.when(held(own, slot))
        def _(slot=slot):
            attend(slot, 1 - side)
            go_y(slot).start()

        if more:
            arrive_and_hand_on(1, slot + 1)
        if slot > 0:
            for kind in range(2):
                send_on(slot - 1, kind)
        send_own(slot)
        if more:
            send_far(slot)

    def gathered(slot):
        @pl.when(held(own, slot))
        def _():
            stay(slot).wait()

        for kind in range(2):
            @pl.when(held(place_of(kind, place_x, 1 - core), slot))
            def _(kind=kind):
                go_c(kind, slot).wait_recv()

            for d in steps:
                from_x = lax.rem(place_x + x_len - d, x_len)

                @pl.when(held(place_of(kind, from_x, 1 - core), slot))
                def _(kind=kind, d=d):
                    go_f(kind, slot, d).wait_recv()

    def let_go(slot):
        @pl.when(held(own, slot))
        def _():
            go_y(slot).wait_send()

        for kind in range(2):
            @pl.when(held(own if kind == 0 else far, slot))
            def _(kind=kind):
                for d in steps:
                    go_x(kind, slot, d).wait_send()
                go_c(kind, slot).wait_send()

            for d in steps:
                @pl.when(held(place_of(kind, lax.rem(place_x + x_len - d, x_len), core), slot))
                def _(kind=kind, d=d):
                    go_f(kind, slot, d).wait_send()

    rows = projected.shape[0]
    width = heads * HEAD

    def product(slot):
        present = [
            start_head(g, places, heads) + slot
            for g in range(places)
            if slot < start_head(g + 1, places, heads) - start_head(g, places, heads)
        ]

        @pl.loop(0, MERGE)
        def _(r):
            at = pl.ds(pl.multiple_of(r * rows, rows), rows)
            left = jnp.concatenate([merged[h, at, :] for h in present], axis=1)
            right = jnp.concatenate(
                [weight[pl.ds(pl.multiple_of(r * width + h * HEAD, HEAD), HEAD), :] for h in present], axis=0
            )
            projected[...] += jnp.dot(left, right, preferred_element_type=jnp.float32)

    send_far(slots - 1)
    load.wait()
    for slot in range(slots - 1):
        gathered(slot)
        product(slot)
    for kind in range(2):
        send_on(slots - 1, kind)
    gathered(slots - 1)
    product(slots - 1)
    for slot in slot_range:
        for a in range(3):
            sent_all(a, slot)
        handed_away(slot)
        let_go(slot)

    values = projected[...]
    lane = lax.broadcasted_iota(jnp.int32, (rows, LANES), 1)
    member = (row_marks[side, pl.ds(0, rows, stride=MERGE), :] > 0.5) & (lane < LANES - 1)
    squares = jnp.sum(values * values, axis=1, keepdims=True)
    tops = jnp.max(values, axis=1, keepdims=True)
    sums = jnp.sum(jnp.where(member, squares, 0.0), axis=0, keepdims=True)
    peaks = jnp.max(jnp.where(member, tops, masked_score), axis=0, keepdims=True)
    counts = jnp.sum(member.astype(jnp.float32), axis=0, keepdims=True) * values.shape[1]
    line = lax.broadcasted_iota(jnp.int32, (8, LANES), 0)

    def spread(stats, tile, me, count, target_of, send, recv):
        stats[me] = tile

        def send_to(d):
            return pltpu.make_async_remote_copy(
                src_ref=stats.at[me], dst_ref=stats.at[me],
                send_sem=send.at[d - 1], recv_sem=recv.at[d - 1],
                device_id=target_of(d), device_id_type=MESH,
            )

        for d in range(1, count):
            send_to(d).start()
        for d in range(1, count):
            send_to(d).wait()
        every = stats[...]
        return jnp.where(line == 1, jnp.max(every, axis=0), jnp.sum(every, axis=0))

    tile = jnp.where(line == 0, sums, jnp.where(line == 1, peaks, counts))
    tile = spread(part_stats, tile, part, tp, lambda d: (blk, lax.rem(part + d, tp)), p_send, p_recv)
    tile = spread(blk_stats, tile, blk, blks, lambda d: (lax.rem(blk + d, blks), part), b_send, b_recv)
    scale = lax.rsqrt(tile[0:1] / jnp.maximum(tile[2:3], 1.0) + epsilon)
    row_scale = jnp.sum(jnp.where(member, scale, 0.0), axis=1, keepdims=True)
    normed_ref[...] = (values * row_scale).astype(jnp.bfloat16)
    peak_ref[...] = (tile[1:2] * scale)[0, :blks]


def per_device(queries, keys, values, segment_ids, proj_weight):
    blks, tp = lax.axis_size("blk"), lax.axis_size("tp")
    width = queries.shape[1]
    heads = width // HEAD
    block_len = segment_ids.shape[0] // blks
    places = 2 * tp
    slots = -(-heads // places)
    peers = places - 1
    pair_len = 2 * block_len
    columns = proj_weight.shape[1]
    dma, anywhere = pltpu.SemaphoreType.DMA, pl.BlockSpec(memory_space=pl.ANY)
    in_vmem = pl.BlockSpec(memory_space=pltpu.VMEM)
    x_len = tp // 2
    merged_rows = block_len // MERGE
    sems = [dma((3, slots, peers))] * 2 + [dma((3, slots))] + [dma((2, slots, 2))] * 2
    sems += [dma(()), dma((slots,)), dma((slots,)), dma((slots,))]
    sems += [dma((2, slots, x_len - 1))] * 2 + [dma((2, slots))] * 2 + [dma((2, slots, x_len - 1))] * 2
    sems += [dma((tp - 1,))] * 2 + [dma((blks - 1,))] * 2
    vmem16 = lambda *shape: pltpu.VMEM(shape, jnp.bfloat16)
    vmem32 = lambda *shape: pltpu.VMEM(shape, jnp.float32)
    normed, peaks = pl.pallas_call(
        functools.partial(whole_kernel, tp, blks, heads, slots, block_len),
        out_shape=[
            jax.ShapeDtypeStruct((merged_rows, columns), jnp.bfloat16),
            jax.ShapeDtypeStruct((blks,), jnp.float32),
        ],
        in_specs=[anywhere, anywhere, anywhere, in_vmem, anywhere],
        out_specs=[in_vmem, in_vmem],
        scratch_shapes=[
            vmem16(slots, pair_len, HEAD),
            vmem16(slots, 2 * pair_len, HEAD),
            vmem16(slots, 2 * pair_len, HEAD),
            vmem16(2 * pair_len, LANES),
            vmem16(pair_len, LANES),
            vmem32(2, block_len, LANES),
            vmem16(slots, 2, block_len, HEAD),
            vmem32(TOGETHER, QUERY_TILE, HEAD),
            vmem16(heads, block_len, HEAD),
            vmem16(*proj_weight.shape),
            vmem32(merged_rows, columns),
            vmem32(tp, 8, LANES),
            vmem32(blks, 8, LANES),
        ] + sems,
        compiler_params=pltpu.CompilerParams(
            collective_id=0, has_side_effects=True, vmem_limit_bytes=56 * 1024 * 1024
        ),
        name="whole",
    )(queries, keys, values, segment_ids[None], proj_weight)
    return normed, peaks


def solution(mesh):
    in_specs = (
        P(("blk", "tp"), None),
        P(("blk", "tp"), None),
        P(("blk", "tp"), None),
        P(),
        P(None, "tp"),
    )
    out_specs = (P("blk", "tp"), P())
    return jax.shard_map(
        per_device, mesh=mesh, in_specs=in_specs, out_specs=out_specs, check_vma=False
    )
```

```python
import functools

import jax
import jax.numpy as jnp
from jax import lax
from jax.experimental import pallas as pl
from jax.experimental.pallas import tpu as pltpu
from jax.sharding import PartitionSpec as P

HEAD = 128
MERGE = 4
QUERY_TILE = 256
KEY_TILE = 768
TOGETHER = 2
LANES = 128
masked_score = -1e30
least_top = -1e20
epsilon = 1e-06
score_scale = HEAD ** (-0.5) * 1.4426950408889634
MESH = pl.DeviceIdType.MESH


def start_head(place, places, heads):
    return (place * heads) // places


def whole_kernel(
    tp, blks, heads, slots, block_len,
    q_in, k_in, v_in, seg_ref, w_ref, normed_ref, peak_ref,
    queries, keys, values_held, key_marks, query_marks, row_marks, o_ref, mixed_ref,
    merged, weight, projected, part_stats, blk_stats,
    send, recv, keep_sem, pass_send, pass_recv,
    w_sem, own_sem, y_send, y_recv, x_send, x_recv, c_send, c_recv, f_send, f_recv,
    p_send, p_recv, b_send, b_recv,
):
    blk, part = lax.axis_index("blk"), lax.axis_index("tp")
    side, place_x, core = lax.rem(blk, 2), part // 2, lax.rem(part, 2)
    pair, pairs = blk // 2, blks // 2
    x_len, places = tp // 2, 2 * tp
    place = side * tp + part
    sibling = (blk, part + 1 - 2 * core)
    across = (blk + 1 - 2 * side, part)
    slab = q_in.shape[0]
    load = pltpu.make_async_copy(w_ref, weight, w_sem)

    barrier = pltpu.get_barrier_semaphore()
    for d in range(1, tp):
        other_part = lax.rem(part + d, tp)
        pl.semaphore_signal(barrier, inc=1, device_id=(blk, other_part), device_id_type=MESH)
        pl.semaphore_signal(barrier, inc=1, device_id=(across[0], other_part), device_id_type=MESH)
    for d in range(1, blks):
        pl.semaphore_signal(barrier, inc=1, device_id=(lax.rem(blk + d, blks), part), device_id_type=MESH)

    has_prev, has_next = pair > 0, pair < pairs - 1

    @pl.when(pair == 0)
    def _():
        for ref in (keys, values_held):
            ref[:, 0:block_len, :] = jnp.zeros((slots, block_len, HEAD), jnp.bfloat16)

    @pl.when(pair == pairs - 1)
    def _():
        for ref in (keys, values_held):
            ref[:, 3 * block_len : 4 * block_len, :] = jnp.zeros((slots, block_len, HEAD), jnp.bfloat16)

    pl.semaphore_wait(barrier, 2 * (tp - 1) + blks - 1)

    def first(place):
        return start_head(place, places, heads)

    def held(place, slot):
        return slot < first(place + 1) - first(place)

    def place_of(kind, to_x, to_core):
        return (side if kind == 0 else 1 - side) * tp + to_x * 2 + to_core

    def copy(src, head, send_sem, recv_sem, target):
        return pltpu.make_async_remote_copy(
            src_ref=src, dst_ref=merged.at[head], send_sem=send_sem, recv_sem=recv_sem,
            device_id=target, device_id_type=MESH,
        )

    own = place_of(0, place_x, core)
    far = place_of(1, place_x, core)

    def clipped(place, slot):
        return jnp.minimum(first(place) + slot, heads - 1)

    def stay(slot):
        return pltpu.make_async_copy(o_ref.at[slot, side], merged.at[clipped(own, slot)], own_sem.at[slot])

    def go_y(slot):
        return copy(o_ref.at[slot, 1 - side], clipped(own, slot), y_send.at[slot], y_recv.at[slot], across)

    def source(kind, slot):
        return o_ref.at[slot, side] if kind == 0 else merged.at[clipped(far, slot)]

    def go_x(kind, slot, d):
        target = (blk, lax.rem(place_x + d, x_len) * 2 + core)
        head = clipped(own if kind == 0 else far, slot)
        return copy(source(kind, slot), head, x_send.at[kind, slot, d - 1], x_recv.at[kind, slot, d - 1], target)

    def go_c(kind, slot):
        head = clipped(own if kind == 0 else far, slot)
        return copy(source(kind, slot), head, c_send.at[kind, slot], c_recv.at[kind, slot], sibling)

    def go_f(kind, slot, d):
        came = clipped(place_of(kind, lax.rem(place_x + x_len - d, x_len), core), slot)
        return copy(merged.at[came], came, f_send.at[kind, slot, d - 1], f_recv.at[kind, slot, d - 1], sibling)

    offsets = [(dy, dt) for dy in (1, 0) for dt in range(tp) if (dy, dt) != (0, 0)]
    arrays = ((k_in, keys, block_len), (v_in, values_held, block_len), (q_in, queries, 0))

    def push(a, slot, i):
        src, dst, base = arrays[a]
        dy, dt = offsets[i]
        to_side, to_part = lax.rem(side + dy, 2), lax.rem(part + dt, tp)
        column = clipped(to_side * tp + to_part, slot) * HEAD
        return pltpu.make_async_remote_copy(
            src_ref=src.at[:, pl.ds(pl.multiple_of(column, HEAD), HEAD)],
            dst_ref=dst.at[slot, pl.ds(pl.multiple_of(base + place * slab, slab), slab), :],
            send_sem=send.at[a, slot, i],
            recv_sem=recv.at[a, slot, i],
            device_id=(pair * 2 + to_side, to_part),
            device_id_type=MESH,
        )

    def pushed_to(slot, i):
        dy, dt = offsets[i]
        return held(lax.rem(side + dy, 2) * tp + lax.rem(part + dt, tp), slot)

    def keep(a, slot):
        src, dst, base = arrays[a]
        return pltpu.make_async_copy(
            src.at[:, pl.ds(pl.multiple_of(clipped(place, slot) * HEAD, HEAD), HEAD)],
            dst.at[slot, pl.ds(pl.multiple_of(base + place * slab, slab), slab), :],
            keep_sem.at[a, slot],
        )

    def hand_on(a, slot, forward):
        dst = arrays[a][1]
        if forward:
            src_rows, dst_rows, target = pl.ds(2 * block_len, block_len), pl.ds(0, block_len), blk + 2
        else:
            src_rows, dst_rows, target = pl.ds(block_len, block_len), pl.ds(3 * block_len, block_len), blk - 2
        return pltpu.make_async_remote_copy(
            src_ref=dst.at[slot, src_rows, :],
            dst_ref=dst.at[slot, dst_rows, :],
            send_sem=pass_send.at[a, slot, forward],
            recv_sem=pass_recv.at[a, slot, forward],
            device_id=(target, part),
            device_id_type=MESH,
        )

    def start_all(a, slot):
        for i in range(len(offsets)):
            @pl.when(pushed_to(slot, i))
            def _(i=i):
                push(a, slot, i).start()

        @pl.when(held(own, slot))
        def _():
            keep(a, slot).start()

    def sent_all(a, slot):
        for i in range(len(offsets)):
            @pl.when(pushed_to(slot, i))
            def _(i=i):
                push(a, slot, i).wait_send()

    def arrive_all(a, slot):
        @pl.when(held(own, slot))
        def _():
            for i in range(len(offsets)):
                push(a, slot, i).wait_recv()
            keep(a, slot).wait()

    def hand_on_all(a, slot):
        @pl.when(held(own, slot) & has_prev)
        def _():
            hand_on(a, slot, 0).start()

        @pl.when(held(own, slot) & has_next)
        def _():
            hand_on(a, slot, 1).start()

    def handed_all(slot):
        for a in range(2):
            @pl.when(held(own, slot) & has_prev)
            def _(a=a):
                hand_on(a, slot, 1).wait_recv()

            @pl.when(held(own, slot) & has_next)
            def _(a=a):
                hand_on(a, slot, 0).wait_recv()

    def handed_away(slot):
        for a in range(2):
            @pl.when(held(own, slot) & has_prev)
            def _(a=a):
                hand_on(a, slot, 0).wait_send()

            @pl.when(held(own, slot) & has_next)
            def _(a=a):
                hand_on(a, slot, 1).wait_send()

    window = 2 * block_len + QUERY_TILE

    def attend(slot, block):
        per_block = block_len // QUERY_TILE
        part_rows = QUERY_TILE // MERGE

        @pl.loop(0, per_block // TOGETHER)
        def _(step):
            tiles = [step * TOGETHER + u for u in range(TOGETHER)]
            ones = jnp.ones((KEY_TILE, HEAD), jnp.bfloat16)

            def parts_of(n):
                begin = pl.multiple_of((block * per_block + n) * QUERY_TILE, QUERY_TILE)
                return begin, [
                    pl.ds(pl.multiple_of(begin + c, QUERY_TILE), KEY_TILE) for c in range(0, window, KEY_TILE)
                ]

            def score(n):
                begin, chunks = parts_of(n)
                rows = pl.ds(begin, QUERY_TILE)
                left = jnp.concatenate([queries[slot, rows, :], query_marks[rows, :]], axis=1)
                return [
                    lax.dot_general(
                        left, jnp.concatenate([keys[slot, c, :], key_marks[c, :]], axis=1),
                        (((1,), (1,)), ((), ())), preferred_element_type=jnp.float32,
                    )
                    for c in chunks
                ]

            def mix(u, n, scores):
                top = functools.reduce(jnp.maximum, [jnp.max(x, axis=1, keepdims=True) for x in scores])
                top = jnp.maximum(top, least_top)
                mixed = jnp.zeros((QUERY_TILE, 2 * HEAD), jnp.float32)
                for x, c in zip(scores, parts_of(n)[1]):
                    terms = jnp.exp2((x - top) * score_scale).astype(jnp.bfloat16)
                    right = jnp.concatenate([values_held[slot, c, :], ones], axis=1)
                    mixed += jnp.dot(terms, right, preferred_element_type=jnp.float32)
                mixed_ref[u] = mixed[:, :HEAD] / jnp.maximum(mixed[:, HEAD:], 1.0)

            ahead = score(tiles[0])
            for u, n in enumerate(tiles):
                scores = ahead
                if u + 1 < TOGETHER:
                    ahead = score(tiles[u + 1])
                mix(u, n, scores)
            for u, n in enumerate(tiles):
                for r in range(MERGE):
                    rows_to = pl.ds(pl.multiple_of(r * (block_len // MERGE) + n * part_rows, part_rows), part_rows)
                    o_ref[slot, block, rows_to, :] = mixed_ref[
                        u, pl.ds(r, part_rows, stride=MERGE), :
                    ].astype(jnp.bfloat16)

    slot_range, steps = range(slots), range(1, x_len)

    def send_own(slot):
        @pl.when(held(own, slot))
        def _():
            for d in steps:
                go_x(0, slot, d).start()
            go_c(0, slot).start()
            stay(slot).start()

    def send_far(slot):
        @pl.when(held(far, slot))
        def _():
            go_y(slot).wait_recv()
            for d in steps:
                go_x(1, slot, d).start()
            go_c(1, slot).start()

    def send_on(slot, kind):
        for d in steps:
            @pl.when(held(place_of(kind, lax.rem(place_x + x_len - d, x_len), core), slot))
            def _(d=d):
                go_x(kind, slot, d).wait_recv()
                go_f(kind, slot, d).start()

    start_all(0, 0)
    start_all(1, 0)
    load.start()

    image = lax.broadcasted_iota(jnp.int32, (LANES, block_len), 0)
    lane = lax.broadcasted_iota(jnp.int32, (block_len, LANES), 1)
    for n in range(4):
        block = pair * 2 - 1 + n
        inside = (block >= 0) & (block < blks)
        from_row = jnp.clip(block, 0, blks - 1) * block_len
        segs = seg_ref[:, pl.ds(pl.multiple_of(from_row, LANES), block_len)]
        segs = jnp.where(inside & (segs >= 0), segs, LANES - 1)
        marks = jnp.where(segs == image, 1.0, 0.0).T
        key_marks[n * block_len : (n + 1) * block_len, :] = marks.astype(jnp.bfloat16)
        if n in (1, 2):
            query_marks[(n - 1) * block_len : n * block_len, :] = jnp.where(
                (marks > 0.5) & (lane < LANES - 1), 0.0, masked_score
            ).astype(jnp.bfloat16)
            row_marks[n - 1] = marks
    projected[...] = jnp.zeros_like(projected)

    def arrive_and_hand_on(a, slot):
        arrive_all(a, slot)
        hand_on_all(a, slot)

    arrive_and_hand_on(0, 0)
    start_all(2, 0)
    arrive_and_hand_on(1, 0)
    if slots > 1:
        start_all(0, 1)
        start_all(1, 1)
    arrive_all(2, 0)
    if slots > 1:
        start_all(2, 1)
    handed_all(0)
    if slots > 1:
        arrive_and_hand_on(0, 1)

    def after_far(slot):
        @pl.when(held(own, slot))
        def _():
            go_y(slot).start()

        if slot + 1 < slots:
            arrive_and_hand_on(1, slot + 1)
        if slot > 0:
            send_far(slot - 1)

    def after_own(slot):
        send_own(slot)
        if slot + 1 < slots:
            arrive_all(2, slot + 1)
            handed_all(slot + 1)

    @pl.loop(0, 2 * slots)
    def _(phase):
        slot = phase // 2

        @pl.when(held(own, slot))
        def _():
            attend(slot, lax.rem(phase + 1 + side, 2))

        for done in slot_range:
            pl.when(phase == 2 * done)(functools.partial(after_far, done))
            pl.when(phase == 2 * done + 1)(functools.partial(after_own, done))

    def gathered(slot):
        @pl.when(held(own, slot))
        def _():
            stay(slot).wait()

        for kind in range(2):
            @pl.when(held(place_of(kind, place_x, 1 - core), slot))
            def _(kind=kind):
                go_c(kind, slot).wait_recv()

            for d in steps:
                from_x = lax.rem(place_x + x_len - d, x_len)

                @pl.when(held(place_of(kind, from_x, 1 - core), slot))
                def _(kind=kind, d=d):
                    go_f(kind, slot, d).wait_recv()

    def let_go(slot):
        @pl.when(held(own, slot))
        def _():
            go_y(slot).wait_send()

        for kind in range(2):
            @pl.when(held(own if kind == 0 else far, slot))
            def _(kind=kind):
                for d in steps:
                    go_x(kind, slot, d).wait_send()
                go_c(kind, slot).wait_send()

            for d in steps:
                @pl.when(held(place_of(kind, lax.rem(place_x + x_len - d, x_len), core), slot))
                def _(kind=kind, d=d):
                    go_f(kind, slot, d).wait_send()

    rows = projected.shape[0]
    width = heads * HEAD

    def product(slot):
        present = [
            start_head(g, places, heads) + slot
            for g in range(places)
            if slot < start_head(g + 1, places, heads) - start_head(g, places, heads)
        ]

        @pl.loop(0, MERGE)
        def _(r):
            at = pl.ds(pl.multiple_of(r * rows, rows), rows)
            left = jnp.concatenate([merged[h, at, :] for h in present], axis=1)
            right = jnp.concatenate(
                [weight[pl.ds(pl.multiple_of(r * width + h * HEAD, HEAD), HEAD), :] for h in present], axis=0
            )
            projected[...] += jnp.dot(left, right, preferred_element_type=jnp.float32)

    send_far(slots - 1)
    load.wait()
    for slot in range(slots - 1):
        for kind in range(2):
            send_on(slot, kind)
        gathered(slot)
        product(slot)
    for kind in range(2):
        send_on(slots - 1, kind)
    gathered(slots - 1)
    product(slots - 1)
    for slot in slot_range:
        for a in range(3):
            sent_all(a, slot)
        handed_away(slot)
        let_go(slot)

    values = projected[...]
    lane = lax.broadcasted_iota(jnp.int32, (rows, LANES), 1)
    member = (row_marks[side, pl.ds(0, rows, stride=MERGE), :] > 0.5) & (lane < LANES - 1)
    squares = jnp.sum(values * values, axis=1, keepdims=True)
    tops = jnp.max(values, axis=1, keepdims=True)
    sums = jnp.sum(jnp.where(member, squares, 0.0), axis=0, keepdims=True)
    peaks = jnp.max(jnp.where(member, tops, masked_score), axis=0, keepdims=True)
    counts = jnp.sum(member.astype(jnp.float32), axis=0, keepdims=True) * values.shape[1]
    line = lax.broadcasted_iota(jnp.int32, (8, LANES), 0)

    def spread(stats, tile, me, count, target_of, send, recv):
        stats[me] = tile

        def send_to(d):
            return pltpu.make_async_remote_copy(
                src_ref=stats.at[me], dst_ref=stats.at[me],
                send_sem=send.at[d - 1], recv_sem=recv.at[d - 1],
                device_id=target_of(d), device_id_type=MESH,
            )

        for d in range(1, count):
            send_to(d).start()
        for d in range(1, count):
            send_to(d).wait()
        every = stats[...]
        return jnp.where(line == 1, jnp.max(every, axis=0), jnp.sum(every, axis=0))

    tile = jnp.where(line == 0, sums, jnp.where(line == 1, peaks, counts))
    tile = spread(part_stats, tile, part, tp, lambda d: (blk, lax.rem(part + d, tp)), p_send, p_recv)
    tile = spread(blk_stats, tile, blk, blks, lambda d: (lax.rem(blk + d, blks), part), b_send, b_recv)
    scale = lax.rsqrt(tile[0:1] / jnp.maximum(tile[2:3], 1.0) + epsilon)
    row_scale = jnp.sum(jnp.where(member, scale, 0.0), axis=1, keepdims=True)
    normed_ref[...] = (values * row_scale).astype(jnp.bfloat16)
    peak_ref[...] = (tile[1:2] * scale)[0, :blks]


def per_device(queries, keys, values, segment_ids, proj_weight):
    blks, tp = lax.axis_size("blk"), lax.axis_size("tp")
    width = queries.shape[1]
    heads = width // HEAD
    block_len = segment_ids.shape[0] // blks
    places = 2 * tp
    slots = -(-heads // places)
    peers = places - 1
    pair_len = 2 * block_len
    columns = proj_weight.shape[1]
    dma, anywhere = pltpu.SemaphoreType.DMA, pl.BlockSpec(memory_space=pl.ANY)
    in_vmem = pl.BlockSpec(memory_space=pltpu.VMEM)
    x_len = tp // 2
    merged_rows = block_len // MERGE
    sems = [dma((3, slots, peers))] * 2 + [dma((3, slots))] + [dma((2, slots, 2))] * 2
    sems += [dma(()), dma((slots,)), dma((slots,)), dma((slots,))]
    sems += [dma((2, slots, x_len - 1))] * 2 + [dma((2, slots))] * 2 + [dma((2, slots, x_len - 1))] * 2
    sems += [dma((tp - 1,))] * 2 + [dma((blks - 1,))] * 2
    vmem16 = lambda *shape: pltpu.VMEM(shape, jnp.bfloat16)
    vmem32 = lambda *shape: pltpu.VMEM(shape, jnp.float32)
    normed, peaks = pl.pallas_call(
        functools.partial(whole_kernel, tp, blks, heads, slots, block_len),
        out_shape=[
            jax.ShapeDtypeStruct((merged_rows, columns), jnp.bfloat16),
            jax.ShapeDtypeStruct((blks,), jnp.float32),
        ],
        in_specs=[anywhere, anywhere, anywhere, in_vmem, anywhere],
        out_specs=[in_vmem, in_vmem],
        scratch_shapes=[
            vmem16(slots, pair_len, HEAD),
            vmem16(slots, 2 * pair_len, HEAD),
            vmem16(slots, 2 * pair_len, HEAD),
            vmem16(2 * pair_len, LANES),
            vmem16(pair_len, LANES),
            vmem32(2, block_len, LANES),
            vmem16(slots, 2, block_len, HEAD),
            vmem32(TOGETHER, QUERY_TILE, HEAD),
            vmem16(heads, block_len, HEAD),
            vmem16(*proj_weight.shape),
            vmem32(merged_rows, columns),
            vmem32(tp, 8, LANES),
            vmem32(blks, 8, LANES),
        ] + sems,
        compiler_params=pltpu.CompilerParams(
            collective_id=0, has_side_effects=True, vmem_limit_bytes=56 * 1024 * 1024
        ),
        name="whole",
    )(queries, keys, values, segment_ids[None], proj_weight)
    return normed, peaks


def solution(mesh):
    in_specs = (
        P(("blk", "tp"), None),
        P(("blk", "tp"), None),
        P(("blk", "tp"), None),
        P(),
        P(None, "tp"),
    )
    out_specs = (P("blk", "tp"), P())
    return jax.shard_map(
        per_device, mesh=mesh, in_specs=in_specs, out_specs=out_specs, check_vma=False
    )
```

```python
import functools

import jax
import jax.numpy as jnp
from jax import lax
from jax.experimental import pallas as pl
from jax.experimental.pallas import tpu as pltpu
from jax.sharding import PartitionSpec as P

HEAD = 128
MERGE = 4
QUERY_TILE = 256
KEY_TILE = 768
TOGETHER = 2
LANES = 128
masked_score = -1e30
least_top = -1e20
epsilon = 1e-06
score_scale = HEAD ** (-0.5) * 1.4426950408889634
MESH = pl.DeviceIdType.MESH


def start_head(place, places, heads):
    return (place * heads) // places


def whole_kernel(
    tp, blks, heads, slots, block_len,
    q_in, k_in, v_in, seg_ref, w_ref, normed_ref, peak_ref,
    queries, keys, values_held, key_marks, query_marks, row_marks, o_ref, mixed_ref,
    merged, weight, projected, part_stats, blk_stats,
    send, recv, keep_sem, pass_send, pass_recv,
    w_sem, own_sem, y_send, y_recv, x_send, x_recv, c_send, c_recv, f_send, f_recv,
    p_send, p_recv, b_send, b_recv,
):
    blk, part = lax.axis_index("blk"), lax.axis_index("tp")
    side, place_x, core = lax.rem(blk, 2), part // 2, lax.rem(part, 2)
    pair, pairs = blk // 2, blks // 2
    x_len, places = tp // 2, 2 * tp
    place = side * tp + part
    sibling = (blk, part + 1 - 2 * core)
    across = (blk + 1 - 2 * side, part)
    slab = q_in.shape[0]
    load = pltpu.make_async_copy(w_ref, weight, w_sem)

    barrier = pltpu.get_barrier_semaphore()
    for d in range(1, tp):
        other_part = lax.rem(part + d, tp)
        pl.semaphore_signal(barrier, inc=1, device_id=(blk, other_part), device_id_type=MESH)
        pl.semaphore_signal(barrier, inc=1, device_id=(across[0], other_part), device_id_type=MESH)
    for d in range(1, blks):
        pl.semaphore_signal(barrier, inc=1, device_id=(lax.rem(blk + d, blks), part), device_id_type=MESH)

    has_prev, has_next = pair > 0, pair < pairs - 1

    @pl.when(pair == 0)
    def _():
        for ref in (keys, values_held):
            ref[:, 0:block_len, :] = jnp.zeros((slots, block_len, HEAD), jnp.bfloat16)

    @pl.when(pair == pairs - 1)
    def _():
        for ref in (keys, values_held):
            ref[:, 3 * block_len : 4 * block_len, :] = jnp.zeros((slots, block_len, HEAD), jnp.bfloat16)

    pl.semaphore_wait(barrier, 2 * (tp - 1) + blks - 1)

    def first(place):
        return start_head(place, places, heads)

    def held(place, slot):
        return slot < first(place + 1) - first(place)

    def place_of(kind, to_x, to_core):
        return (side if kind == 0 else 1 - side) * tp + to_x * 2 + to_core

    def copy(src, head, send_sem, recv_sem, target):
        return pltpu.make_async_remote_copy(
            src_ref=src, dst_ref=merged.at[head], send_sem=send_sem, recv_sem=recv_sem,
            device_id=target, device_id_type=MESH,
        )

    own = place_of(0, place_x, core)
    far = place_of(1, place_x, core)

    def clipped(place, slot):
        return jnp.minimum(first(place) + slot, heads - 1)

    def stay(slot):
        return pltpu.make_async_copy(o_ref.at[slot, side], merged.at[clipped(own, slot)], own_sem.at[slot])

    def go_y(slot):
        return copy(o_ref.at[slot, 1 - side], clipped(own, slot), y_send.at[slot], y_recv.at[slot], across)

    def source(kind, slot):
        return o_ref.at[slot, side] if kind == 0 else merged.at[clipped(far, slot)]

    def go_x(kind, slot, d):
        target = (blk, lax.rem(place_x + d, x_len) * 2 + core)
        head = clipped(own if kind == 0 else far, slot)
        return copy(source(kind, slot), head, x_send.at[kind, slot, d - 1], x_recv.at[kind, slot, d - 1], target)

    def go_c(kind, slot):
        head = clipped(own if kind == 0 else far, slot)
        return copy(source(kind, slot), head, c_send.at[kind, slot], c_recv.at[kind, slot], sibling)

    def go_f(kind, slot, d):
        came = clipped(place_of(kind, lax.rem(place_x + x_len - d, x_len), core), slot)
        return copy(merged.at[came], came, f_send.at[kind, slot, d - 1], f_recv.at[kind, slot, d - 1], sibling)

    offsets = [(dy, dt) for dy in (1, 0) for dt in range(tp) if (dy, dt) != (0, 0)]
    arrays = ((k_in, keys, block_len), (v_in, values_held, block_len), (q_in, queries, 0))

    def push(a, slot, i):
        src, dst, base = arrays[a]
        dy, dt = offsets[i]
        to_side, to_part = lax.rem(side + dy, 2), lax.rem(part + dt, tp)
        column = clipped(to_side * tp + to_part, slot) * HEAD
        return pltpu.make_async_remote_copy(
            src_ref=src.at[:, pl.ds(pl.multiple_of(column, HEAD), HEAD)],
            dst_ref=dst.at[slot, pl.ds(pl.multiple_of(base + place * slab, slab), slab), :],
            send_sem=send.at[a, slot, i],
            recv_sem=recv.at[a, slot, i],
            device_id=(pair * 2 + to_side, to_part),
            device_id_type=MESH,
        )

    def pushed_to(slot, i):
        dy, dt = offsets[i]
        return held(lax.rem(side + dy, 2) * tp + lax.rem(part + dt, tp), slot)

    def keep(a, slot):
        src, dst, base = arrays[a]
        return pltpu.make_async_copy(
            src.at[:, pl.ds(pl.multiple_of(clipped(place, slot) * HEAD, HEAD), HEAD)],
            dst.at[slot, pl.ds(pl.multiple_of(base + place * slab, slab), slab), :],
            keep_sem.at[a, slot],
        )

    def hand_on(a, slot, forward):
        dst = arrays[a][1]
        if forward:
            src_rows, dst_rows, target = pl.ds(2 * block_len, block_len), pl.ds(0, block_len), blk + 2
        else:
            src_rows, dst_rows, target = pl.ds(block_len, block_len), pl.ds(3 * block_len, block_len), blk - 2
        return pltpu.make_async_remote_copy(
            src_ref=dst.at[slot, src_rows, :],
            dst_ref=dst.at[slot, dst_rows, :],
            send_sem=pass_send.at[a, slot, forward],
            recv_sem=pass_recv.at[a, slot, forward],
            device_id=(target, part),
            device_id_type=MESH,
        )

    def start_all(a, slot):
        for i in range(len(offsets)):
            @pl.when(pushed_to(slot, i))
            def _(i=i):
                push(a, slot, i).start()

        @pl.when(held(own, slot))
        def _():
            keep(a, slot).start()

    def sent_all(a, slot):
        for i in range(len(offsets)):
            @pl.when(pushed_to(slot, i))
            def _(i=i):
                push(a, slot, i).wait_send()

    def arrive_all(a, slot):
        @pl.when(held(own, slot))
        def _():
            for i in range(len(offsets)):
                push(a, slot, i).wait_recv()
            keep(a, slot).wait()

    def hand_on_all(a, slot):
        @pl.when(held(own, slot) & has_prev)
        def _():
            hand_on(a, slot, 0).start()

        @pl.when(held(own, slot) & has_next)
        def _():
            hand_on(a, slot, 1).start()

    def handed_all(slot):
        for a in range(2):
            @pl.when(held(own, slot) & has_prev)
            def _(a=a):
                hand_on(a, slot, 1).wait_recv()

            @pl.when(held(own, slot) & has_next)
            def _(a=a):
                hand_on(a, slot, 0).wait_recv()

    def handed_away(slot):
        for a in range(2):
            @pl.when(held(own, slot) & has_prev)
            def _(a=a):
                hand_on(a, slot, 0).wait_send()

            @pl.when(held(own, slot) & has_next)
            def _(a=a):
                hand_on(a, slot, 1).wait_send()

    window = 2 * block_len + QUERY_TILE

    def attend(slot, block):
        per_block = block_len // QUERY_TILE
        part_rows = QUERY_TILE // MERGE

        @pl.loop(0, per_block // TOGETHER)
        def _(step):
            tiles = [step * TOGETHER + u for u in range(TOGETHER)]
            at, chunks, scores = [], [], []
            for n in tiles:
                begin = pl.multiple_of((block * per_block + n) * QUERY_TILE, QUERY_TILE)
                rows = pl.ds(begin, QUERY_TILE)
                left = jnp.concatenate([queries[slot, rows, :], query_marks[rows, :]], axis=1)
                mine = [pl.ds(pl.multiple_of(begin + c, QUERY_TILE), KEY_TILE) for c in range(0, window, KEY_TILE)]
                chunks.append(mine)
                scores.append([
                    lax.dot_general(
                        left, jnp.concatenate([keys[slot, c, :], key_marks[c, :]], axis=1),
                        (((1,), (1,)), ((), ())), preferred_element_type=jnp.float32,
                    )
                    for c in mine
                ])
            ones = jnp.ones((KEY_TILE, HEAD), jnp.bfloat16)
            for u, n in enumerate(tiles):
                top = functools.reduce(jnp.maximum, [jnp.max(x, axis=1, keepdims=True) for x in scores[u]])
                top = jnp.maximum(top, least_top)
                mixed = jnp.zeros((QUERY_TILE, 2 * HEAD), jnp.float32)
                for x, c in zip(scores[u], chunks[u]):
                    terms = jnp.exp2((x - top) * score_scale).astype(jnp.bfloat16)
                    right = jnp.concatenate([values_held[slot, c, :], ones], axis=1)
                    mixed += jnp.dot(terms, right, preferred_element_type=jnp.float32)
                mixed_ref[u] = mixed[:, :HEAD] / jnp.maximum(mixed[:, HEAD:], 1.0)
            for u, n in enumerate(tiles):
                for r in range(MERGE):
                    rows_to = pl.ds(pl.multiple_of(r * (block_len // MERGE) + n * part_rows, part_rows), part_rows)
                    o_ref[slot, block, rows_to, :] = mixed_ref[
                        u, pl.ds(r, part_rows, stride=MERGE), :
                    ].astype(jnp.bfloat16)

    slot_range, steps = range(slots), range(1, x_len)

    def send_own(slot):
        @pl.when(held(own, slot))
        def _():
            attend(slot, side)
            for d in steps:
                go_x(0, slot, d).start()
            go_c(0, slot).start()
            stay(slot).start()

    def send_far(slot):
        @pl.when(held(far, slot))
        def _():
            go_y(slot).wait_recv()
            for d in steps:
                go_x(1, slot, d).start()
            go_c(1, slot).start()

    def send_on(slot, kind):
        for d in steps:
            @pl.when(held(place_of(kind, lax.rem(place_x + x_len - d, x_len), core), slot))
            def _(d=d):
                go_x(kind, slot, d).wait_recv()
                go_f(kind, slot, d).start()

    for a in range(3):
        start_all(a, 0)
    load.start()

    image = lax.broadcasted_iota(jnp.int32, (LANES, block_len), 0)
    lane = lax.broadcasted_iota(jnp.int32, (block_len, LANES), 1)
    for n in range(4):
        block = pair * 2 - 1 + n
        inside = (block >= 0) & (block < blks)
        from_row = jnp.clip(block, 0, blks - 1) * block_len
        segs = seg_ref[:, pl.ds(pl.multiple_of(from_row, LANES), block_len)]
        segs = jnp.where(inside & (segs >= 0), segs, LANES - 1)
        marks = jnp.where(segs == image, 1.0, 0.0).T
        key_marks[n * block_len : (n + 1) * block_len, :] = marks.astype(jnp.bfloat16)
        if n in (1, 2):
            query_marks[(n - 1) * block_len : n * block_len, :] = jnp.where(
                (marks > 0.5) & (lane < LANES - 1), 0.0, masked_score
            ).astype(jnp.bfloat16)
            row_marks[n - 1] = marks
    projected[...] = jnp.zeros_like(projected)

    for slot in slot_range:
        for a in range(3):
            arrive_all(a, slot)
            if a < 2:
                hand_on_all(a, slot)
            if slot + 1 < slots:
                start_all(a, slot + 1)
        handed_all(slot)
        if slot > 0:
            send_far(slot - 1)

        @pl.when(held(own, slot))
        def _(slot=slot):
            attend(slot, 1 - side)
            go_y(slot).start()

        if slot > 0:
            for kind in range(2):
                send_on(slot - 1, kind)
        send_own(slot)
    def gathered(slot):
        @pl.when(held(own, slot))
        def _():
            stay(slot).wait()

        for kind in range(2):
            @pl.when(held(place_of(kind, place_x, 1 - core), slot))
            def _(kind=kind):
                go_c(kind, slot).wait_recv()

            for d in steps:
                from_x = lax.rem(place_x + x_len - d, x_len)

                @pl.when(held(place_of(kind, from_x, 1 - core), slot))
                def _(kind=kind, d=d):
                    go_f(kind, slot, d).wait_recv()

    def let_go(slot):
        @pl.when(held(own, slot))
        def _():
            go_y(slot).wait_send()

        for kind in range(2):
            @pl.when(held(own if kind == 0 else far, slot))
            def _(kind=kind):
                for d in steps:
                    go_x(kind, slot, d).wait_send()
                go_c(kind, slot).wait_send()

            for d in steps:
                @pl.when(held(place_of(kind, lax.rem(place_x + x_len - d, x_len), core), slot))
                def _(kind=kind, d=d):
                    go_f(kind, slot, d).wait_send()

    rows = projected.shape[0]
    width = heads * HEAD

    def product(slot):
        present = [
            start_head(g, places, heads) + slot
            for g in range(places)
            if slot < start_head(g + 1, places, heads) - start_head(g, places, heads)
        ]

        @pl.loop(0, MERGE)
        def _(r):
            at = pl.ds(pl.multiple_of(r * rows, rows), rows)
            left = jnp.concatenate([merged[h, at, :] for h in present], axis=1)
            right = jnp.concatenate(
                [weight[pl.ds(pl.multiple_of(r * width + h * HEAD, HEAD), HEAD), :] for h in present], axis=0
            )
            projected[...] += jnp.dot(left, right, preferred_element_type=jnp.float32)

    send_far(slots - 1)
    load.wait()
    for slot in range(slots - 1):
        gathered(slot)
        product(slot)
    for kind in range(2):
        send_on(slots - 1, kind)
    gathered(slots - 1)
    product(slots - 1)
    for slot in slot_range:
        for a in range(3):
            sent_all(a, slot)
        handed_away(slot)
        let_go(slot)

    values = projected[...]
    lane = lax.broadcasted_iota(jnp.int32, (rows, LANES), 1)
    member = (row_marks[side, pl.ds(0, rows, stride=MERGE), :] > 0.5) & (lane < LANES - 1)
    squares = jnp.sum(values * values, axis=1, keepdims=True)
    tops = jnp.max(values, axis=1, keepdims=True)
    sums = jnp.sum(jnp.where(member, squares, 0.0), axis=0, keepdims=True)
    peaks = jnp.max(jnp.where(member, tops, masked_score), axis=0, keepdims=True)
    counts = jnp.sum(member.astype(jnp.float32), axis=0, keepdims=True) * values.shape[1]
    line = lax.broadcasted_iota(jnp.int32, (8, LANES), 0)

    def spread(stats, tile, me, count, target_of, send, recv):
        stats[me] = tile

        def send_to(d):
            return pltpu.make_async_remote_copy(
                src_ref=stats.at[me], dst_ref=stats.at[me],
                send_sem=send.at[d - 1], recv_sem=recv.at[d - 1],
                device_id=target_of(d), device_id_type=MESH,
            )

        for d in range(1, count):
            send_to(d).start()
        for d in range(1, count):
            send_to(d).wait()
        every = stats[...]
        return jnp.where(line == 1, jnp.max(every, axis=0), jnp.sum(every, axis=0))

    tile = jnp.where(line == 0, sums, jnp.where(line == 1, peaks, counts))
    tile = spread(part_stats, tile, part, tp, lambda d: (blk, lax.rem(part + d, tp)), p_send, p_recv)
    tile = spread(blk_stats, tile, blk, blks, lambda d: (lax.rem(blk + d, blks), part), b_send, b_recv)
    scale = lax.rsqrt(tile[0:1] / jnp.maximum(tile[2:3], 1.0) + epsilon)
    row_scale = jnp.sum(jnp.where(member, scale, 0.0), axis=1, keepdims=True)
    normed_ref[...] = (values * row_scale).astype(jnp.bfloat16)
    peak_ref[...] = (tile[1:2] * scale)[0, :blks]


def per_device(queries, keys, values, segment_ids, proj_weight):
    blks, tp = lax.axis_size("blk"), lax.axis_size("tp")
    width = queries.shape[1]
    heads = width // HEAD
    block_len = segment_ids.shape[0] // blks
    places = 2 * tp
    slots = -(-heads // places)
    peers = places - 1
    pair_len = 2 * block_len
    columns = proj_weight.shape[1]
    dma, anywhere = pltpu.SemaphoreType.DMA, pl.BlockSpec(memory_space=pl.ANY)
    in_vmem = pl.BlockSpec(memory_space=pltpu.VMEM)
    x_len = tp // 2
    merged_rows = block_len // MERGE
    sems = [dma((3, slots, peers))] * 2 + [dma((3, slots))] + [dma((2, slots, 2))] * 2
    sems += [dma(()), dma((slots,)), dma((slots,)), dma((slots,))]
    sems += [dma((2, slots, x_len - 1))] * 2 + [dma((2, slots))] * 2 + [dma((2, slots, x_len - 1))] * 2
    sems += [dma((tp - 1,))] * 2 + [dma((blks - 1,))] * 2
    vmem16 = lambda *shape: pltpu.VMEM(shape, jnp.bfloat16)
    vmem32 = lambda *shape: pltpu.VMEM(shape, jnp.float32)
    normed, peaks = pl.pallas_call(
        functools.partial(whole_kernel, tp, blks, heads, slots, block_len),
        out_shape=[
            jax.ShapeDtypeStruct((merged_rows, columns), jnp.bfloat16),
            jax.ShapeDtypeStruct((blks,), jnp.float32),
        ],
        in_specs=[in_vmem, in_vmem, in_vmem, in_vmem, anywhere],
        out_specs=[in_vmem, in_vmem],
        scratch_shapes=[
            vmem16(slots, pair_len, HEAD),
            vmem16(slots, 2 * pair_len, HEAD),
            vmem16(slots, 2 * pair_len, HEAD),
            vmem16(2 * pair_len, LANES),
            vmem16(pair_len, LANES),
            vmem32(2, block_len, LANES),
            vmem16(slots, 2, block_len, HEAD),
            vmem32(TOGETHER, QUERY_TILE, HEAD),
            vmem16(heads, block_len, HEAD),
            vmem16(*proj_weight.shape),
            vmem32(merged_rows, columns),
            vmem32(tp, 8, LANES),
            vmem32(blks, 8, LANES),
        ] + sems,
        compiler_params=pltpu.CompilerParams(
            collective_id=0, has_side_effects=True, vmem_limit_bytes=56 * 1024 * 1024
        ),
        name="whole",
    )(queries, keys, values, segment_ids[None], proj_weight)
    return normed, peaks


def solution(mesh):
    in_specs = (
        P(("blk", "tp"), None),
        P(("blk", "tp"), None),
        P(("blk", "tp"), None),
        P(),
        P(None, "tp"),
    )
    out_specs = (P("blk", "tp"), P())
    return jax.shard_map(
        per_device, mesh=mesh, in_specs=in_specs, out_specs=out_specs, check_vma=False
    )
```
